32 devices in a mesh: leaf: 8 (over z, y), near: 4 (over x, core).
Axes of the slice: x: 2, y: 2, z: 4, core: 2. Of those that a mesh axis runs over, the one named last changes fastest.
Arguments:
- bases: float32 [64, 64, 64], P('leaf'), may hold values from -1 to 4
- leaf_transfer: float32 [64, 64, 64], P('leaf'), may hold values from -1 to 4
- top_transfer: float32 [32, 64, 64], P('leaf'), may hold values from -1 to 4
- couplings: bfloat16 [4096, 64, 64], P(('leaf', 'near')), may hold values from -6 to 6
- coupling_target: int32 [4096], P(('leaf', 'near')), may hold values from 0 to 7
- coupling_dest: int32 [4096, 1], P(('leaf', 'near')), may hold values from 0 to 7; in each aligned block of 128 rows (0 to 127, 128 to 255, ...) at most 32 rows name the same one
- coupling_local: int32 [4096], P(('leaf', 'near')), may hold values from 0 to 7
- top_couplings: bfloat16 [512, 64, 64], P(('leaf', 'near')), may hold values from -0.59765625 to 0.59765625
- top_target: int32 [512], P(('leaf', 'near')), may hold values from 0 to 7
- top_source: int32 [512], P(('leaf', 'near')), may hold values from 0 to 15
Outputs:
- leaf_bases: float32 [64, 64, 64], P(('leaf', 'near'))
- leaf_transfers: float32 [64, 64, 64], P('leaf')
- top_transfers: float32 [32, 64, 64], P('leaf')
- new_couplings: bfloat16 [4096, 64, 64], P(('leaf', 'near'))
- new_top_couplings: bfloat16 [512, 64, 64], P(('leaf', 'near'))
The draws below stay inside these ranges and needn't reach their ends.
Inputs may be any that keep to these rules, and one draw needn't show every extreme that they name: `coupling_dest`: among the leaf blocks of one device, at most 32 have their source in the same subtree.
All inputs are finite; a program needn't handle non-finite values.
Results may differ from the reference program's by a relative error of at most 0.0065.
Values may be sent and summed in bfloat16 or wider, within the bound.
No kernel may reach another device: no remote copies, remote signals or barrier semaphores. Data moves between devices by JAX's collectives and lax.ppermute only.
A program may use at most 128 MiB of HBM per device.

```python
import math
import jax
import jax.numpy as jnp
import numpy as np
from jax import lax

RANK = 64
LEAF_PTS = 64
LEAF_DEV = 8
BLK_DEV = 128
TOP_DEV = 16
CAP = 32
LEAVES = 64
MIDS = 32
TOPS = 16
ROWS = 4096
TOP_ROWS = 512
N_LEAF = 8
N_NEAR = 4


def dominant(key, batch_count, row_count, col_count):
    key_diagonal, key_rest = jax.random.split(key)
    spread_scale = 0.6 / math.sqrt(col_count)
    diagonal = jax.random.uniform(key_diagonal, (batch_count, 1, col_count), jnp.float32, 1.0, 2.0)
    off_diagonal = jnp.clip(jax.random.normal(key_rest, (batch_count, row_count, col_count), jnp.float32), -4.0, 4.0)
    identity = jnp.eye(row_count, col_count, dtype=jnp.float32)
    return identity * diagonal + spread_scale * off_diagonal


def draw_bases(key, part):
    return dominant(jax.random.fold_in(key, 11), LEAVES, LEAF_PTS, RANK)


def draw_leaf_transfer(key, part):
    return dominant(jax.random.fold_in(key, 23), LEAVES, RANK, RANK)


def draw_top_transfer(key, part):
    return dominant(jax.random.fold_in(key, 37), MIDS, RANK, RANK)


def touch_ends(array, stream_key, least, high):
    shape = array.shape
    spot = [jax.random.randint(jax.random.fold_in(stream_key, axis), (), 0, shape[axis]) for axis in range(len(shape))]
    array = array.at[tuple(spot)].set(least)
    longest = shape.index(max(shape))
    spot[longest] = (spot[longest] + 1) % shape[longest]
    return array.at[tuple(spot)].set(high)


def levels(rng, shape, cuts, smallest, largest):
    def one(dim, shards_of):
        draws = jax.random.uniform(jax.random.fold_in(jax.random.fold_in(rng, 6), dim), (shards_of,), jnp.float32, smallest / len(cuts), largest / len(cuts))
        return jnp.repeat(jnp.exp(draws), shape[dim] // shards_of).reshape((-1,) + (1,) * (len(shape) - dim - 1))

    gain = one(*cuts[0])
    for cut in cuts[1:]:
        gain = gain * one(*cut)
    return gain


def assign_block(own_key, own, number, rows, amount, top, limit, slope):
    order = jax.random.permutation(own_key, amount)
    crowded, common = load_shares(amount, rows * top, limit, slope, True), load_shares(amount, rows * top, limit, slope, False)
    places = jnp.arange(amount)

    def named(lengths, offset_by):
        used = int((lengths > 0).sum())
        fixed = max(1, used // 4)
        moved = fixed + (places - fixed + offset_by * (used - fixed)) % max(1, amount - fixed)
        return jnp.zeros((amount,), jnp.int32).at[order[jnp.where(places < fixed, places, moved)]].set(jnp.asarray(lengths, jnp.int32))

    lengths = jnp.where(number % 4 == 0, named(crowded, number // 4), named(common, number - number // 4 - 1))
    mixed = jax.random.permutation(jax.random.fold_in(own, 3), amount)
    giver, receiver = mixed[0:amount // 2 * 2:2], mixed[1:amount // 2 * 2:2]
    slack = jnp.minimum(lengths[giver] - 1, limit - lengths[receiver]) // 2
    slack = jnp.where((giver == order[0]) | (receiver == order[0]) | (lengths[receiver] == 0), 0, jnp.maximum(slack, 0))
    moved = jax.random.randint(jax.random.fold_in(own, 4), (amount // 2,), 0, 1 << 20) % (slack + 1)
    lengths = lengths.at[giver].add(-moved).at[receiver].add(moved)
    items = jnp.searchsorted(jnp.cumsum(lengths), jnp.arange(rows * top), side="right").astype(jnp.int32)
    grid = items.reshape(top, rows).T
    grid = grid[jax.random.permutation(jax.random.fold_in(own, 1), rows)]
    offset_by = jax.random.randint(jax.random.fold_in(own, 2), (rows, 1), 0, top)
    return jnp.take_along_axis(grid, (jnp.arange(top)[None, :] + offset_by) % top, axis=1)


def load_shares(amount, total, most, slope, full):
    portions = [(1 << 20) // math.isqrt(grade ** slope) + 1 for grade in range(1, amount + 1)]
    largest = most if full else min(most, max(-(-total // amount), total * portions[0] // sum(portions)))
    least = 1 if total - largest >= amount - 1 else 0
    holding, surplus = [largest] + [least] * (amount - 1), total - largest - least * (amount - 1)
    while surplus > 0:
        movable = [i for i in range(1, amount) if holding[i] < largest] or [i for i in range(1, amount) if holding[i] < most]
        mass, left = sum([portions[i] for i in movable]), surplus
        for i in movable:
            more = min(most - holding[i], max(1, left * portions[i] // mass), surplus)
            holding[i] = holding[i] + more
            surplus = surplus - more
    return np.array(holding)


def bell_draw(own_key, dims, scale, bound, cuts=(), kind=jnp.bfloat16):
    array = jax.random.normal(own_key, dims, jnp.float32) * scale
    if len(cuts) > 0:
        array = levels(own_key, dims, cuts, -0.22, 0.18) * array
    return jnp.clip(array, min=-bound, max=bound).astype(kind)


def setup_inputs(seed: int = 0) -> dict:
    seeds = jax.random.split(jax.random.key(seed), 11)
    bases = draw_bases(jax.random.fold_in(seeds[10], 71), 0)
    leaf_transfer = draw_leaf_transfer(jax.random.fold_in(seeds[10], 71), 0)
    top_transfer = draw_top_transfer(jax.random.fold_in(seeds[10], 71), 0)
    couplings = bell_draw(seeds[3], (ROWS, RANK, RANK), 1.0, 6.0, ((0, 32),))
    coupling_target = touch_ends(jax.random.randint(seeds[4], (ROWS,), 0, LEAF_DEV), jax.random.fold_in(seeds[4], 1), 0, LEAF_DEV - 1).astype(jnp.int32)
    coupling_dest_keys = jax.random.split(jax.random.fold_in(seeds[5], 1), ROWS // BLK_DEV)
    coupling_dest_turns = jax.random.permutation(jax.random.fold_in(seeds[5], 3), ROWS // BLK_DEV)
    coupling_dest = jax.vmap(lambda own, number: assign_block(jax.random.fold_in(seeds[5], 2), own, number, BLK_DEV, N_LEAF, 1, CAP, 2))(coupling_dest_keys, coupling_dest_turns).reshape((ROWS, 1))
    coupling_local = touch_ends(jax.random.randint(seeds[6], (ROWS,), 0, LEAF_DEV), jax.random.fold_in(seeds[6], 1), 0, LEAF_DEV - 1).astype(jnp.int32)
    top_couplings = bell_draw(seeds[7], (TOP_ROWS, RANK, RANK), 0.1, 0.59765625, ((0, 32),))
    top_target = touch_ends(jax.random.randint(seeds[8], (TOP_ROWS,), 0, LEAF_DEV), jax.random.fold_in(seeds[8], 1), 0, LEAF_DEV - 1).astype(jnp.int32)
    top_source = touch_ends(jax.random.randint(seeds[9], (TOP_ROWS,), 0, TOPS), jax.random.fold_in(seeds[9], 1), 0, TOPS - 1).astype(jnp.int32)
    return dict(bases=bases, leaf_transfer=leaf_transfer, top_transfer=top_transfer, couplings=couplings, coupling_target=coupling_target, coupling_dest=coupling_dest, coupling_local=coupling_local, top_couplings=top_couplings, top_target=top_target, top_source=top_source)


exact_mode = lax.Precision.HIGHEST

def gram_of(stacked):
    return jnp.einsum('nmk,nml->nkl', stacked, stacked, precision=exact_mode)

def right_solve(lower_part, stacked):

    def single(factor_one, block_one):
        return jax.scipy.linalg.solve_triangular(factor_one, block_one.T, lower=True).T
    return jax.vmap(single)(lower_part, stacked)

def merge_level(pieces, groups, width):
    paired = pieces.reshape(groups, 2, width, RANK, RANK)
    first_child = paired[:, 0].reshape(groups * width, RANK, RANK)
    second_child = paired[:, 1].reshape(groups * width, RANK, RANK)
    lower_part = jnp.linalg.cholesky(gram_of(first_child) + gram_of(second_child))
    spread = jnp.broadcast_to(lower_part.reshape(groups, 1, width, RANK, RANK), paired.shape)
    transfers = right_solve(spread.reshape(-1, RANK, RANK), pieces)
    return (transfers, jnp.swapaxes(lower_part, 1, 2))

def project(table, target_ids, source_ids, blocks, per_group):
    count = blocks.shape[0] // per_group

    def one_group(inputs):
        targets, sources, block_set = inputs
        left_rows = table[targets].astype(jnp.float32)
        right_rows = table[sources].astype(jnp.float32)
        halves = jnp.einsum('nkr,nrl->nkl', left_rows, block_set.astype(jnp.float32)).astype(jnp.bfloat16)
        return jnp.einsum('nkr,nlr->nkl', halves.astype(jnp.float32), right_rows).astype(jnp.bfloat16)
    result = lax.map(one_group, (target_ids.reshape(count, per_group), source_ids.reshape(count, per_group), blocks.reshape(count, per_group, RANK, RANK)))
    return result.reshape(blocks.shape)

def reference(bases, leaf_transfer, top_transfer, couplings, coupling_target, coupling_dest, coupling_local, top_couplings, top_target, top_source):
    lower_leaf = jnp.linalg.cholesky(gram_of(bases))
    leaf_bases = right_solve(lower_leaf, bases)
    leaf_factor = jnp.swapaxes(lower_leaf, 1, 2)
    child_piece = jnp.einsum('nkr,nrl->nkl', leaf_factor, leaf_transfer, precision=exact_mode)
    leaf_transfers, mid_factor = merge_level(child_piece, N_LEAF // 2, LEAF_DEV)
    up_piece = jnp.einsum('nkr,nrl->nkl', mid_factor, top_transfer, precision=exact_mode)
    top_transfers, top_factor = merge_level(up_piece, N_LEAF // 4, LEAF_DEV)
    leaf_low = leaf_factor.astype(jnp.bfloat16)
    top_low = top_factor.astype(jnp.bfloat16)
    row_index = jnp.arange(couplings.shape[0], dtype=jnp.int32)
    subtree = row_index // (N_NEAR * BLK_DEV)
    leaf_targets = subtree * LEAF_DEV + coupling_target
    leaf_sources = coupling_dest[:, 0] * LEAF_DEV + coupling_local
    new_couplings = project(leaf_low, leaf_targets, leaf_sources, couplings, BLK_DEV)
    top_index = jnp.arange(top_couplings.shape[0], dtype=jnp.int32)
    top_subtree = top_index // (N_NEAR * TOP_DEV)
    top_targets = top_subtree // 4 * LEAF_DEV + top_target
    new_top_couplings = project(top_low, top_targets, top_source, top_couplings, TOP_DEV)
    return (leaf_bases, leaf_transfers, top_transfers, new_couplings, new_top_couplings)
```

```python
import functools

import jax
import jax.numpy as jnp
from jax import lax
from jax.experimental import pallas as pl
from jax.experimental.pallas import tpu as pltpu
from jax.sharding import PartitionSpec as P

exact = lax.Precision.HIGHEST
f32 = jnp.float32
bf16 = jnp.bfloat16
BLOCK = 8
VMEM_LIMIT = 48 * 2**20


def swapped(value, axis, mask):
    pairs = [(source, source ^ mask) for source in range(lax.axis_size(axis))]
    return lax.ppermute(value, axis, pairs)


def gathered_by_xor(value, axis, bits):
    for bit in bits:
        value = jnp.concatenate([value, swapped(value, axis, 1 << bit)], axis=0)
    return value


def place_of(difference, bits):
    place = jnp.zeros_like(difference)
    for order, bit in enumerate(bits):
        place = place | (((difference >> bit) & 1) << order)
    return place


def dot_nn(a, b):
    return jnp.dot(a, b, precision=exact, preferred_element_type=f32)


def dot_tn(a, b):
    return lax.dot_general(a, b, (((0,), (0,)), ((), ())), precision=exact, preferred_element_type=f32)


def dot_nt(a, b):
    return lax.dot_general(a, b, (((1,), (1,)), ((), ())), precision=exact, preferred_element_type=f32)


def low_nn(a, b):
    return jnp.dot(a, b, preferred_element_type=f32).astype(bf16)


def low_nt(a, b):
    return lax.dot_general(a, b, (((1,), (1,)), ((), ())), preferred_element_type=f32).astype(bf16)


def across(rows, lane):
    return jnp.broadcast_to(rows[:, lane : lane + 1], rows.shape)


def reciprocal(value):
    guess = pltpu.reciprocal(value, approx=True)
    return guess * (2.0 - value * guess)


def square_places(rank):
    return (
        lax.broadcasted_iota(jnp.int32, (rank, rank), 0),
        lax.broadcasted_iota(jnp.int32, (rank, rank), 1),
    )


def put_matrix(work, place, gram):
    rank = gram.shape[0]
    rows, columns = square_places(rank)
    identity = (rows == columns).astype(f32)
    work[pl.ds(place, rank, stride=8), :] = jnp.concatenate([gram, identity], axis=1)


def eliminate(work, rank):
    def read(i):
        return work[i * 8 : (i + 1) * 8, :]

    for start in range(0, rank, BLOCK):
        rows = [read(start + a) for a in range(BLOCK)]
        entry = [[across(rows[a], start + b) if b >= a else None for b in range(BLOCK)] for a in range(BLOCK)]
        inverse = []
        for a in range(BLOCK):
            inverse.append(reciprocal(entry[a][a]))
            for b in range(a + 1, BLOCK):
                share = entry[a][b] * inverse[a]
                for c in range(b, BLOCK):
                    entry[b][c] = entry[b][c] - share * entry[a][c]
                rows[b] = rows[b] - share * rows[a]
        for a in range(1, BLOCK):
            work[(start + a) * 8 : (start + a + 1) * 8, :] = rows[a]
        scaled = [rows[a] * inverse[a] for a in range(BLOCK)]
        for i in range(start + BLOCK, rank):
            total = read(i)
            for a in range(BLOCK):
                total = total - across(scaled[a], i) * rows[a]
            work[i * 8 : (i + 1) * 8, :] = total


def take_matrix(work, place, rank):
    rows, columns = square_places(rank)
    both = work[pl.ds(place, rank, stride=8), :]
    diagonal = jnp.sum(jnp.where(rows == columns, both[:, :rank], 0.0), axis=1, keepdims=True)
    both = both * lax.rsqrt(diagonal)
    factor = jnp.where(columns >= rows, both[:, :rank], 0.0)
    return factor, both[:, rank:]


def leaf_kernel(bases, transfer, low, low_pairs, piece, gram, inverse, work):
    count, _, rank = bases.shape
    for b in range(count):
        put_matrix(work, b, dot_tn(bases[b], bases[b]))
    eliminate(work, rank)
    for pair in range(count // 2):
        grams, lows = [], []
        for b in (2 * pair, 2 * pair + 1):
            factor, inverse_part = take_matrix(work, b, rank)
            child = dot_nn(factor, transfer[b])
            piece[b] = child
            inverse[b] = inverse_part
            low[b] = factor.astype(bf16)
            lows.append(factor)
            grams.append(dot_tn(child, child))
        gram[pair] = jnp.concatenate(grams, axis=1)
        low_pairs[pair] = jnp.concatenate(lows, axis=1).astype(bf16)


def put_sums(work, mine, other, rank):
    for pair in range(mine.shape[0]):
        total = mine[pair] + other[pair]
        put_matrix(work, 2 * pair, total[:, :rank])
        put_matrix(work, 2 * pair + 1, total[:, rank:])


def middle_kernel(spot, mine, other, piece, top_mine, top_other, transfers, up, gram, work):
    count, _, rank = piece.shape
    half = count // 2
    put_sums(work, mine, other, rank)
    eliminate(work, rank)
    near, parity = spot[0], spot[1]
    grams = []
    for slot in range(count):
        place = (slot % half) + half * (parity if slot < half else 1 - parity)
        factor, inverse_part = take_matrix(work, place, rank)
        transfers[place] = dot_nt(piece[place], inverse_part)
        raised = dot_nn(factor, (top_mine if slot < half else top_other)[slot % half])
        if slot < half:
            up[slot] = raised
        grams.append(dot_tn(raised, raised))
        if slot % 2:
            gram[slot // 2] = jnp.concatenate(grams[-2:], axis=1)


def top_kernel(mine, other, up, transfers, low_pairs, work):
    half, _, rank = up.shape
    put_sums(work, mine, other, rank)
    eliminate(work, rank)
    lows = []
    for slot in range(2 * half):
        factor, inverse_part = take_matrix(work, slot, rank)
        if slot < half:
            transfers[slot] = dot_nt(up[slot], inverse_part)
        lows.append(factor)
        if slot % 2:
            low_pairs[slot // 2] = jnp.concatenate(lows[-2:], axis=1).astype(bf16)


def half_kernel(spot, target, source, couplings, low, bases, inverse, halves, leaf_bases):
    count, rank, _ = couplings.shape
    share = leaf_bases.shape[0]
    for k in range(share):
        place = spot[0] * share + k
        leaf_bases[k] = dot_nt(bases[place], inverse[place])

    def step(r, carry):
        product = low_nn(low[target[r]], couplings[r])
        odd = source[r] % 2
        halves[r, :, :rank] = jnp.where(odd == 0, product, jnp.zeros_like(product))
        halves[r, :, rank:] = jnp.where(odd == 1, product, jnp.zeros_like(product))
        return carry

    lax.fori_loop(0, count, step, 0, unroll=8)


def full_kernel(source, halves, table, out):
    count = halves.shape[0]

    def step(r, carry):
        out[r] = low_nt(halves[r], table[source[r] // 2])
        return carry

    lax.fori_loop(0, count, step, 0, unroll=8)


def top_project_kernel(target, source, couplings, table, out):
    count, rank, _ = couplings.shape
    for r in range(count):
        left, right = table[target[r] // 2], table[source[r] // 2]
        left = jnp.where(target[r] % 2 == 0, left[:, :rank], left[:, rank:])
        right = jnp.where(source[r] % 2 == 0, right[:, :rank], right[:, rank:])
        out[r] = low_nt(low_nn(left, couplings[r]), right)


vmem = pl.BlockSpec(memory_space=pltpu.VMEM)
smem = pl.BlockSpec(memory_space=pltpu.SMEM)


def call(kernel, scalars, arrays, outs, scratch=()):
    return pl.pallas_call(
        kernel,
        out_shape=[jax.ShapeDtypeStruct(shape, dtype) for shape, dtype in outs],
        in_specs=[smem] * len(scalars) + [vmem] * len(arrays),
        out_specs=[vmem] * len(outs),
        scratch_shapes=list(scratch),
        compiler_params=pltpu.CompilerParams(vmem_limit_bytes=VMEM_LIMIT),
    )(*scalars, *arrays)


def on_device(
    bases,
    leaf_transfer,
    top_transfer,
    couplings,
    coupling_target,
    coupling_dest,
    coupling_local,
    top_couplings,
    top_target,
    top_source,
):
    leaves, _, rank = bases.shape
    half, pairs = leaves // 2, leaves // 2
    share = leaves // lax.axis_size("near")
    blocks, top_blocks = couplings.shape[0], top_couplings.shape[0]
    leaf_bits = list(range(lax.axis_size("leaf").bit_length() - 1))[::-1]
    quad_bits = [bit - 2 for bit in leaf_bits if bit >= 2]
    near_place, leaf_place = lax.axis_index("near"), lax.axis_index("leaf")
    parity = leaf_place % 2
    spot = jnp.stack([near_place, parity]).astype(jnp.int32)
    work = [pltpu.VMEM((8 * rank, 2 * rank), f32)]
    square = (rank, rank)
    wide = (rank, 2 * rank)

    source = place_of(coupling_dest[:, 0] ^ leaf_place, leaf_bits) * leaves + coupling_local
    top_left = top_target ^ (half * parity)
    top_right = place_of((top_source // leaves) ^ (leaf_place // 4), quad_bits) * leaves + (
        (top_source % leaves) ^ (half * parity)
    )

    top_other = swapped(top_transfer, "leaf", 1)
    low, low_pairs, piece, gram, inverse = call(
        leaf_kernel,
        [],
        [bases, leaf_transfer],
        [
            ((leaves, *square), bf16),
            ((pairs, *wide), bf16),
            ((leaves, *square), f32),
            ((pairs, *wide), f32),
            ((leaves, *square), f32),
        ],
        work,
    )
    gram_other = swapped(gram, "leaf", 1)
    halves, leaf_bases = call(
        half_kernel,
        [spot, coupling_target, source],
        [couplings, low, bases, inverse],
        [((blocks, *wide), bf16), ((share, *square), f32)],
    )
    table = gathered_by_xor(low_pairs, "leaf", leaf_bits)
    leaf_transfers, up, up_gram = call(
        middle_kernel,
        [spot],
        [gram, gram_other, piece, top_transfer, top_other],
        [((leaves, *square), f32), ((half, *square), f32), ((pairs, *wide), f32)],
        work,
    )
    up_other = swapped(up_gram, "leaf", 2)
    top_transfers, top_pairs = call(
        top_kernel,
        [],
        [up_gram, up_other, up],
        [((half, *square), f32), ((pairs, *wide), bf16)],
        work,
    )
    top_table = gathered_by_xor(top_pairs, "leaf", [bit + 2 for bit in quad_bits])
    (new_couplings,) = call(
        full_kernel, [source], [halves, table], [((blocks, *square), bf16)]
    )
    (new_top_couplings,) = call(
        top_project_kernel,
        [top_left, top_right],
        [top_couplings, top_table],
        [((top_blocks, *square), bf16)],
    )
    return (leaf_bases, leaf_transfers, top_transfers, new_couplings, new_top_couplings)


def solution(mesh):
    in_specs = (
        P("leaf", None, None),
        P("leaf", None, None),
        P("leaf", None, None),
        P(("leaf", "near"), None, None),
        P(("leaf", "near")),
        P(("leaf", "near"), None),
        P(("leaf", "near")),
        P(("leaf", "near"), None, None),
        P(("leaf", "near")),
        P(("leaf", "near")),
    )
    out_specs = (
        P(("leaf", "near"), None, None),
        P("leaf", None, None),
        P("leaf", None, None),
        P(("leaf", "near"), None, None),
        P(("leaf", "near"), None, None),
    )
    return jax.shard_map(
        on_device, mesh=mesh, in_specs=in_specs, out_specs=out_specs, check_vma=False
    )
```

```python
import functools

import jax
import jax.numpy as jnp
from jax import lax
from jax.experimental import pallas as pl
from jax.experimental.pallas import tpu as pltpu
from jax.sharding import PartitionSpec as P

exact = lax.Precision.HIGHEST
f32 = jnp.float32
bf16 = jnp.bfloat16
BLOCK = 8
GROUP = 4
PITCH_EXTRA = 8
VMEM_LIMIT = 48 * 2**20


def swapped(value, axis, mask):
    pairs = [(source, source ^ mask) for source in range(lax.axis_size(axis))]
    return lax.ppermute(value, axis, pairs)


def gathered_by_xor(value, axis, bits):
    values = [value]
    for bit in bits:
        values = values + [swapped(one, axis, 1 << bit) for one in values]
    return values


def place_of(difference, bits):
    place = jnp.zeros_like(difference)
    for order, bit in enumerate(bits):
        place = place | (((difference >> bit) & 1) << order)
    return place


def dot_nn(a, b):
    return jnp.dot(a, b, precision=exact, preferred_element_type=f32)


def dot_tn(a, b):
    return lax.dot_general(a, b, (((0,), (0,)), ((), ())), precision=exact, preferred_element_type=f32)


def dot_nt(a, b):
    return lax.dot_general(a, b, (((1,), (1,)), ((), ())), precision=exact, preferred_element_type=f32)


def low_nn(a, b):
    return jnp.dot(a, b, preferred_element_type=f32)


def low_nt(a, b):
    return lax.dot_general(a, b, (((1,), (1,)), ((), ())), preferred_element_type=f32)


def eliminate(work, factor, inverse):
    rank = work.shape[1] // 2
    shape = (2 * GROUP, 2 * rank)
    lanes = lax.broadcasted_iota(jnp.int32, shape, 1)
    odd = lax.broadcasted_iota(jnp.int32, shape, 0) // GROUP
    upper = odd == 0
    column = lanes % rank
    side = lanes - column

    def pick(rows, index):
        return jnp.take_along_axis(rows, index, axis=1)

    def span(pair):
        return pl.ds(2 * GROUP * pair, 2 * GROUP)

    for start in range(0, rank, BLOCK):
        inside = (column >= start) & (column < start + BLOCK)
        rows = []
        for pair in range(start // 2, (start + BLOCK) // 2):
            both = work[span(pair), :]
            turned = pltpu.roll(both, GROUP, axis=0)
            rows += [jnp.where(upper, both, turned), jnp.where(upper, turned, both)]
        done = [(column == start + a).astype(f32) for a in range(BLOCK)]
        entry = [[pick(rows[a], side + (start + b)) if b >= a else None for b in range(BLOCK)] for a in range(BLOCK)]
        scaled = []
        for a in range(BLOCK):
            pivot = pltpu.reciprocal(entry[a][a], approx=True)
            scaled.append(rows[a] * pivot)
            for b in range(a + 1, BLOCK):
                share = entry[a][b] * pivot
                for c in range(b, BLOCK):
                    entry[b][c] = entry[b][c] - share * entry[a][c]
                rows[b] = rows[b] - share * rows[a]
                done[b] = done[b] - share * done[a]
        mixed = [jnp.where(inside, done[a], rows[a]) for a in range(BLOCK)]
        for pair in range((start + BLOCK) // 2, rank // 2):
            total = jnp.where(inside, 0.0, work[span(pair), :])
            index = side + odd + 2 * pair
            for a in range(BLOCK):
                total = total - pick(scaled[a], index) * mixed[a]
            work[span(pair), :] = total
        for a in range(0, BLOCK, 2):
            pair = (start + a) // 2
            row = odd + 2 * pair
            scale = lax.rsqrt(jnp.where(upper, entry[a][a], entry[a + 1][a + 1]))
            factor[span(pair), :] = jnp.where(
                column >= row, jnp.where(upper, rows[a], rows[a + 1]) * scale, 0.0
            )
            inverse[span(pair), :] = jnp.where(
                column <= row, jnp.where(upper, mixed[a], mixed[a + 1]) * scale, 0.0
            )


def matrix_pair(work, group):
    return pl.ds(group, work.shape[1] // 2, stride=GROUP)


def side_by_side(left, right):
    return jnp.concatenate([left, right], axis=1)


def leaf_kernel(bases_far, transfer_far, low, piece, gram, inverse_out, bases, transfer, work, factor, inverse, arrived):
    rank = bases.shape[2]
    first = pltpu.make_async_copy(bases_far, bases, arrived.at[0])
    second = pltpu.make_async_copy(transfer_far, transfer, arrived.at[1])
    first.start()
    second.start()
    first.wait()
    for g in range(GROUP):
        left, right = bases[g], bases[g + GROUP]
        work[matrix_pair(work, g), :] = side_by_side(dot_tn(left, left), dot_tn(right, right))
    eliminate(work, factor, inverse)
    second.wait()
    for g in range(GROUP):
        both = factor[matrix_pair(work, g), :]
        left = dot_nn(both[:, :rank], transfer[g])
        right = dot_nn(both[:, rank:], transfer[g + GROUP])
        piece[g] = left
        piece[g + GROUP] = right
        gram[g] = side_by_side(dot_tn(left, left), dot_tn(right, right))
        low[g] = both.astype(bf16)
        inverse_out[g] = inverse[matrix_pair(work, g), :]


def middle_kernel(spot, mine, other, top_mine, top_other, after, up, gram, inverse_out, work, factor, inverse):
    rank = top_mine.shape[2]
    for g in range(GROUP):
        work[matrix_pair(work, g), :] = mine[g] + other[g]
    eliminate(work, factor, inverse)
    for g in range(GROUP):
        both = factor[matrix_pair(work, g), :]
        both = jnp.where(spot[1] == 0, both, pltpu.roll(both, rank, axis=1))
        left = dot_nn(both[:, :rank], top_mine[g])
        right = dot_nn(both[:, rank:], top_other[g])
        up[g] = left
        gram[g] = side_by_side(dot_tn(left, left), dot_tn(right, right))
        inverse_out[g] = inverse[matrix_pair(work, g), :]


def top_kernel(mine, other, after, low, inverse_out, work, factor, inverse):
    for g in range(GROUP):
        work[matrix_pair(work, g), :] = mine[g] + other[g]
    eliminate(work, factor, inverse)
    for g in range(GROUP):
        low[g] = factor[matrix_pair(work, g), :].astype(bf16)
        inverse_out[g] = inverse[matrix_pair(work, g), :]


def half_kernel(target, couplings, low, halves, turned, table):
    rank, _, count = couplings.shape
    pitch = turned.shape[0] // rank
    for g in range(GROUP):
        both = low[g]
        table[g] = both[:, :rank]
        table[g + GROUP] = both[:, rank:]
    for m in range(rank):
        turned[m * pitch : m * pitch + count, :] = couplings[m].astype(f32).T
    for r in range(count):
        block = turned[pl.ds(r, rank, stride=pitch), :].astype(bf16)
        halves[r] = low_nn(table[target[r]], block).astype(bf16)


def leaf_output_kernel(spot, bases, inverse, piece, middle_inverse, leaf_bases, leaf_transfers):
    rank = bases.shape[2]
    share = leaf_bases.shape[0]
    for k in range(share):
        place = spot[0] * share + k
        both = inverse[place % GROUP]
        both = jnp.where(place < GROUP, both[:, :rank], both[:, rank:])
        leaf_bases[k] = dot_nt(bases[place], both)
    for g in range(GROUP):
        both = middle_inverse[g]
        leaf_transfers[g] = dot_nt(piece[g], both[:, :rank])
        leaf_transfers[g + GROUP] = dot_nt(piece[g + GROUP], both[:, rank:])


def unpack(packed, table, base):
    rank = table.shape[2]
    for g in range(GROUP):
        both = packed[g]
        table[base + g] = both[:, :rank]
        table[base + g + GROUP] = both[:, rank:]


def full_kernel(source, halves, up, inverse, *rest):
    packed, (out, top_transfers, turned, table) = rest[:-4], rest[-4:]
    count, rank, _ = halves.shape
    pitch = turned.shape[0] // rank
    for place, one in enumerate(packed):
        unpack(one, table, 2 * GROUP * place)
    for r in range(count):
        turned[pl.ds(r, rank, stride=pitch), :] = low_nt(halves[r], table[source[r]])
    for g in range(GROUP):
        top_transfers[g] = dot_nt(up[g], inverse[g][:, :rank])
    for k in range(rank):
        out[k] = turned[k * pitch : k * pitch + count, :].T.astype(bf16)


def top_project_kernel(target, source, couplings, after, *rest):
    packed, (out, table) = rest[:-2], rest[-2:]
    count, rank, _ = couplings.shape
    for place, one in enumerate(packed):
        unpack(one, table, 2 * GROUP * place)
    for r in range(count):
        part = low_nn(table[target[r]], couplings[r]).astype(bf16)
        out[r] = low_nt(part, table[source[r]]).astype(bf16)


vmem = pl.BlockSpec(memory_space=pltpu.VMEM)
smem = pl.BlockSpec(memory_space=pltpu.SMEM)
anywhere = pl.BlockSpec(memory_space=pl.ANY)


def call(kernel, outs, scalars=(), arrays=(), after=(), tables=(), scratch=(), far=()):
    return pl.pallas_call(
        kernel,
        out_shape=[jax.ShapeDtypeStruct(shape, dtype) for shape, dtype in outs],
        in_specs=[smem] * len(scalars)
        + [anywhere] * len(far)
        + [vmem] * len(arrays)
        + [anywhere] * len(after)
        + [vmem] * len(tables),
        out_specs=[vmem] * len(outs),
        scratch_shapes=list(scratch),
        compiler_params=pltpu.CompilerParams(vmem_limit_bytes=VMEM_LIMIT),
    )(*scalars, *far, *arrays, *after, *tables)


def on_device(
    bases,
    leaf_transfer,
    top_transfer,
    couplings,
    coupling_target,
    coupling_dest,
    coupling_local,
    top_couplings,
    top_target,
    top_source,
):
    leaves, _, rank = bases.shape
    share = leaves // lax.axis_size("near")
    blocks, top_blocks = couplings.shape[0], top_couplings.shape[0]
    leaf_bits = list(range(lax.axis_size("leaf").bit_length() - 1))[::-1]
    quad_bits = [bit - 2 for bit in leaf_bits if bit >= 2]
    near_place, leaf_place = lax.axis_index("near"), lax.axis_index("leaf")
    parity = leaf_place % 2
    spot = jnp.stack([near_place, parity]).astype(jnp.int32)
    square = (rank, rank)
    packed = (GROUP, rank, 2 * rank)
    work = [pltpu.VMEM((rank * GROUP, 2 * rank), f32)] * 3
    turned = pltpu.VMEM((rank * (blocks + PITCH_EXTRA), rank), f32)

    source = place_of(coupling_dest[:, 0] ^ leaf_place, leaf_bits) * leaves + coupling_local
    top_left = top_target ^ (GROUP * parity)
    top_right = place_of((top_source // leaves) ^ (leaf_place // 4), quad_bits) * leaves + (
        (top_source % leaves) ^ (GROUP * parity)
    )

    top_other = swapped(top_transfer, "leaf", 1)
    low, piece, gram, inverse = call(
        leaf_kernel,
        [(packed, bf16), ((leaves, *square), f32), (packed, f32), (packed, f32)],
        far=[bases, leaf_transfer],
        scratch=[pltpu.VMEM(bases.shape, f32), pltpu.VMEM(leaf_transfer.shape, f32), *work, pltpu.SemaphoreType.DMA((2,))],
    )
    gram_other = swapped(gram, "leaf", 1)
    (halves,) = call(
        half_kernel,
        [((blocks, *square), bf16)],
        scalars=[coupling_target],
        arrays=[jnp.transpose(couplings, (1, 2, 0)), low],
        scratch=[turned, pltpu.VMEM((leaves, *square), bf16)],
    )
    tables = gathered_by_xor(low, "leaf", leaf_bits)
    up, up_gram, middle_inverse = call(
        middle_kernel,
        [((GROUP, *square), f32), (packed, f32), (packed, f32)],
        scalars=[spot],
        arrays=[gram, gram_other, top_transfer, top_other],
        after=[halves],
        scratch=work,
    )
    up_other = swapped(up_gram, "leaf", 2)
    leaf_bases, leaf_transfers = call(
        leaf_output_kernel,
        [((share, *square), f32), ((leaves, *square), f32)],
        scalars=[spot],
        arrays=[bases, inverse, piece, middle_inverse],
    )
    top_low, top_inverse = call(
        top_kernel,
        [(packed, bf16), (packed, f32)],
        arrays=[up_gram, up_other],
        after=[leaf_transfers],
        scratch=work,
    )
    top_tables = gathered_by_xor(top_low, "leaf", [bit + 2 for bit in quad_bits])
    new_couplings, top_transfers = call(
        full_kernel,
        [((rank, rank, blocks), bf16), ((GROUP, *square), f32)],
        scalars=[source],
        arrays=[halves, up, top_inverse],
        tables=tables,
        scratch=[turned, pltpu.VMEM((len(tables) * leaves, *square), bf16)],
    )
    (new_top_couplings,) = call(
        top_project_kernel,
        [((top_blocks, *square), bf16)],
        scalars=[top_left, top_right],
        arrays=[top_couplings],
        after=[new_couplings],
        tables=top_tables,
        scratch=[pltpu.VMEM((len(top_tables) * leaves, *square), bf16)],
    )
    new_couplings = jnp.transpose(new_couplings, (2, 0, 1))
    return (leaf_bases, leaf_transfers, top_transfers, new_couplings, new_top_couplings)


def solution(mesh):
    in_specs = (
        P("leaf", None, None),
        P("leaf", None, None),
        P("leaf", None, None),
        P(("leaf", "near"), None, None),
        P(("leaf", "near")),
        P(("leaf", "near"), None),
        P(("leaf", "near")),
        P(("leaf", "near"), None, None),
        P(("leaf", "near")),
        P(("leaf", "near")),
    )
    out_specs = (
        P(("leaf", "near"), None, None),
        P("leaf", None, None),
        P("leaf", None, None),
        P(("leaf", "near"), None, None),
        P(("leaf", "near"), None, None),
    )
    return jax.shard_map(
        on_device, mesh=mesh, in_specs=in_specs, out_specs=out_specs, check_vma=False
    )
```

```python
import functools

import jax
import jax.numpy as jnp
from jax import lax
from jax.experimental import pallas as pl
from jax.experimental.pallas import tpu as pltpu
from jax.sharding import PartitionSpec as P

exact = lax.Precision.HIGHEST
f32 = jnp.float32
bf16 = jnp.bfloat16
BLOCK = 8
GROUP = 4
PITCH_EXTRA = 8
CHUNKS = 4
VMEM_LIMIT = 48 * 2**20
FLOPS = 1e9


def swapped(value, axis, mask):
    pairs = [(source, source ^ mask) for source in range(lax.axis_size(axis))]
    return lax.ppermute(value, axis, pairs)


def gathered_by_xor(value, axis, bits):
    for step, bit in enumerate(bits):
        other = swapped(value, axis, 1 << bit)
        if step == len(bits) - 1:
            return [value, other]
        value = joined(value, other)
    return [value]


def join_kernel(first, second, out):
    out[: first.shape[0]] = first[...]
    out[first.shape[0] :] = second[...]


def joined(first, second):
    shape = (first.shape[0] + second.shape[0], *first.shape[1:])
    return call(join_kernel, [(shape, first.dtype)], 0.5, arrays=[first, second])[0]


def place_of(difference, bits):
    place = jnp.zeros_like(difference)
    for order, bit in enumerate(bits):
        place = place | (((difference >> bit) & 1) << order)
    return place


def dot_nn(a, b):
    return jnp.dot(a, b, precision=exact, preferred_element_type=f32)


def dot_tn(a, b):
    return lax.dot_general(a, b, (((0,), (0,)), ((), ())), precision=exact, preferred_element_type=f32)


def dot_nt(a, b):
    return lax.dot_general(a, b, (((1,), (1,)), ((), ())), precision=exact, preferred_element_type=f32)


def low_nn(a, b):
    return jnp.dot(a, b, preferred_element_type=f32)


def low_nt(a, b):
    return lax.dot_general(a, b, (((1,), (1,)), ((), ())), preferred_element_type=f32)


def eliminate(work, factor, inverse):
    rank = work.shape[1] // 2
    shape = (2 * GROUP, 2 * rank)
    lanes = lax.broadcasted_iota(jnp.int32, shape, 1)
    odd = lax.broadcasted_iota(jnp.int32, shape, 0) // GROUP
    upper = odd == 0
    column = lanes % rank
    side = lanes - column

    def pick(rows, index):
        return jnp.take_along_axis(rows, index, axis=1)

    def span(pair):
        return pl.ds(2 * GROUP * pair, 2 * GROUP)

    for start in range(0, rank, BLOCK):
        inside = (column >= start) & (column < start + BLOCK)
        rows = []
        for pair in range(start // 2, (start + BLOCK) // 2):
            both = work[span(pair), :]
            turned = pltpu.roll(both, GROUP, axis=0)
            rows += [jnp.where(upper, both, turned), jnp.where(upper, turned, both)]
        done = [(column == start + a).astype(f32) for a in range(BLOCK)]
        entry = [[pick(rows[a], side + (start + b)) if b >= a else None for b in range(BLOCK)] for a in range(BLOCK)]
        scaled = []
        for a in range(BLOCK):
            pivot = pltpu.reciprocal(entry[a][a], approx=True)
            scaled.append(rows[a] * pivot)
            for b in range(a + 1, BLOCK):
                share = entry[a][b] * pivot
                for c in range(b, BLOCK):
                    entry[b][c] = entry[b][c] - share * entry[a][c]
                rows[b] = rows[b] - share * rows[a]
                done[b] = done[b] - share * done[a]
        mixed = [jnp.where(inside, done[a], rows[a]) for a in range(BLOCK)]
        for pair in range((start + BLOCK) // 2, rank // 2):
            total = jnp.where(inside, 0.0, work[span(pair), :])
            index = side + odd + 2 * pair
            for a in range(BLOCK):
                total = total - pick(scaled[a], index) * mixed[a]
            work[span(pair), :] = total
        for a in range(0, BLOCK, 2):
            pair = (start + a) // 2
            row = odd + 2 * pair
            scale = lax.rsqrt(jnp.where(upper, entry[a][a], entry[a + 1][a + 1]))
            factor[span(pair), :] = jnp.where(
                column >= row, jnp.where(upper, rows[a], rows[a + 1]) * scale, 0.0
            )
            inverse[span(pair), :] = jnp.where(
                column <= row, jnp.where(upper, mixed[a], mixed[a + 1]) * scale, 0.0
            )


def matrix_pair(work, group):
    return pl.ds(group, work.shape[1] // 2, stride=GROUP)


def side_by_side(left, right):
    return jnp.concatenate([left, right], axis=1)


def leaf_kernel(bases_far, transfer_far, low, piece, gram, inverse_out, bases, transfer, work, factor, inverse, arrived):
    rank = bases.shape[2]
    first = pltpu.make_async_copy(bases_far, bases, arrived.at[0])
    second = pltpu.make_async_copy(transfer_far, transfer, arrived.at[1])
    first.start()
    second.start()
    first.wait()
    for g in range(GROUP):
        left, right = bases[g], bases[g + GROUP]
        work[matrix_pair(work, g), :] = side_by_side(dot_tn(left, left), dot_tn(right, right))
    eliminate(work, factor, inverse)
    second.wait()
    for g in range(GROUP):
        both = factor[matrix_pair(work, g), :]
        left = dot_nn(both[:, :rank], transfer[g])
        right = dot_nn(both[:, rank:], transfer[g + GROUP])
        piece[g] = left
        piece[g + GROUP] = right
        gram[g] = side_by_side(dot_tn(left, left), dot_tn(right, right))
        low[g] = both.astype(bf16)
        inverse_out[g] = inverse[matrix_pair(work, g), :]


def middle_kernel(spot, mine, other, top_mine, top_other, token, up, gram, inverse_out, work, factor, inverse):
    rank = top_mine.shape[2]
    for g in range(GROUP):
        work[matrix_pair(work, g), :] = mine[g] + other[g]
    eliminate(work, factor, inverse)
    for g in range(GROUP):
        both = factor[matrix_pair(work, g), :]
        both = jnp.where(spot[1] == 0, both, pltpu.roll(both, rank, axis=1))
        left = dot_nn(both[:, :rank], top_mine[g])
        right = dot_nn(both[:, rank:], top_other[g])
        up[g] = left
        gram[g] = side_by_side(dot_tn(left, left), dot_tn(right, right))
        inverse_out[g] = inverse[matrix_pair(work, g), :]


def top_kernel(mine, other, token, low, inverse_out, work, factor, inverse):
    for g in range(GROUP):
        work[matrix_pair(work, g), :] = mine[g] + other[g]
    eliminate(work, factor, inverse)
    for g in range(GROUP):
        low[g] = factor[matrix_pair(work, g), :].astype(bf16)
        inverse_out[g] = inverse[matrix_pair(work, g), :]


def half_kernel(target, couplings_far, low, halves, token, couplings, turned, table, arrived):
    rank, _, count = couplings.shape
    pitch = turned.shape[0] // rank
    token[...] = jnp.zeros_like(token)
    chunk = rank // CHUNKS
    copies = []
    for k in range(CHUNKS):
        part = pl.ds(k * chunk, chunk)
        copies.append(pltpu.make_async_copy(couplings_far.at[part], couplings.at[part], arrived.at[k]))
        copies[k].start()
    for g in range(GROUP):
        both = low[g]
        table[g] = both[:, :rank]
        table[g + GROUP] = both[:, rank:]
    for k in range(CHUNKS):
        copies[k].wait()
        for m in range(k * chunk, (k + 1) * chunk):
            turned[m * pitch : m * pitch + count, :] = couplings[m].astype(f32).T
    for r in range(count):
        block = turned[pl.ds(r, rank, stride=pitch), :].astype(bf16)
        halves[r] = low_nn(table[target[r]], block).astype(bf16)


def leaf_output_kernel(spot, bases_far, inverse, piece, middle_inverse, leaf_bases, leaf_transfers, token, bases, arrived):
    share, _, rank = bases.shape
    token[...] = jnp.zeros_like(token)
    copy = pltpu.make_async_copy(bases_far.at[pl.ds(spot[0] * share, share)], bases, arrived)
    copy.start()
    for g in range(GROUP):
        both = middle_inverse[g]
        leaf_transfers[g] = dot_nt(piece[g], both[:, :rank])
        leaf_transfers[g + GROUP] = dot_nt(piece[g + GROUP], both[:, rank:])
    copy.wait()
    for k in range(share):
        place = spot[0] * share + k
        both = inverse[place % GROUP]
        both = jnp.where(place < GROUP, both[:, :rank], both[:, rank:])
        leaf_bases[k] = dot_nt(bases[k], both)


def unpack(packed, table, base):
    count, rank = packed.shape[0], table.shape[2]

    def step(n, carry):
        both = packed[n]
        place = base + 2 * GROUP * (n // GROUP) + n % GROUP
        table[place] = both[:, :rank]
        table[place + GROUP] = both[:, rank:]
        return carry

    lax.fori_loop(0, count, step, 0, unroll=min(count, 16))


def full_kernel(
    source,
    target,
    top_far,
    halves,
    up,
    inverse,
    top_low,
    *rest,
):
    packed, rest = rest[:-11], rest[-11:]
    out_far, top_transfers, top_halves, token = rest[:4]
    out, turned, table, top_couplings, top_table, arrived, left = rest[4:]
    count, rank, _ = halves.shape
    pitch = turned.shape[0] // rank
    token[...] = jnp.zeros_like(token)
    copy = pltpu.make_async_copy(top_far, top_couplings, arrived)
    copy.start()
    base = 0
    for one in packed:
        unpack(one, table, base)
        base += 2 * one.shape[0]
    for r in range(count):
        turned[pl.ds(r, rank, stride=pitch), :] = low_nt(halves[r], table[source[r]])
    chunk = rank // CHUNKS
    copies = []
    for k in range(CHUNKS):
        for m in range(k * chunk, (k + 1) * chunk):
            out[m] = turned[m * pitch : m * pitch + count, :].T.astype(bf16)
        part = pl.ds(k * chunk, chunk)
        copies.append(pltpu.make_async_copy(out.at[part], out_far.at[part], left.at[k]))
        copies[k].start()
    unpack(top_low, top_table, 0)
    for g in range(GROUP):
        top_transfers[g] = dot_nt(up[g], inverse[g][:, :rank])
    copy.wait()
    for r in range(top_couplings.shape[0]):
        top_halves[r] = low_nn(top_table[target[r]], top_couplings[r]).astype(bf16)
    for copy in copies:
        copy.wait()


def top_project_kernel(source, halves, token, *rest):
    packed, (out, table) = rest[:-2], rest[-2:]
    base = 0
    for one in packed:
        unpack(one, table, base)
        base += 2 * one.shape[0]
    for r in range(halves.shape[0]):
        out[r] = low_nt(halves[r], table[source[r]]).astype(bf16)


vmem = pl.BlockSpec(memory_space=pltpu.VMEM)
smem = pl.BlockSpec(memory_space=pltpu.SMEM)
hbm = pl.BlockSpec(memory_space=pltpu.HBM)


def call(kernel, outs, microseconds, scalars=(), far=(), arrays=(), scratch=(), far_outs=0):
    return pl.pallas_call(
        kernel,
        out_shape=[jax.ShapeDtypeStruct(shape, dtype) for shape, dtype in outs],
        in_specs=[smem] * len(scalars) + [hbm] * len(far) + [vmem] * len(arrays),
        out_specs=[hbm] * far_outs + [vmem] * (len(outs) - far_outs),
        scratch_shapes=list(scratch),
        compiler_params=pltpu.CompilerParams(vmem_limit_bytes=VMEM_LIMIT),
        cost_estimate=pl.CostEstimate(flops=int(microseconds * FLOPS), bytes_accessed=0, transcendentals=0),
    )(*scalars, *far, *arrays)


def on_device(
    bases,
    leaf_transfer,
    top_transfer,
    couplings,
    coupling_target,
    coupling_dest,
    coupling_local,
    top_couplings,
    top_target,
    top_source,
):
    leaves, _, rank = bases.shape
    share = leaves // lax.axis_size("near")
    blocks, top_blocks = couplings.shape[0], top_couplings.shape[0]
    leaf_bits = list(range(lax.axis_size("leaf").bit_length() - 1))[::-1]
    quad_bits = [bit - 2 for bit in leaf_bits if bit >= 2]
    near_place, leaf_place = lax.axis_index("near"), lax.axis_index("leaf")
    parity = leaf_place % 2
    spot = jnp.stack([near_place, parity]).astype(jnp.int32)
    square = (rank, rank)
    packed = (GROUP, rank, 2 * rank)
    work = [pltpu.VMEM((rank * GROUP, 2 * rank), f32)] * 3
    turned = pltpu.VMEM((rank * (blocks + PITCH_EXTRA), rank), f32)

    source = place_of(coupling_dest[:, 0] ^ leaf_place, leaf_bits) * leaves + coupling_local
    top_left = top_target ^ (GROUP * parity)
    top_right = place_of((top_source // leaves) ^ (leaf_place // 4), quad_bits) * leaves + (
        (top_source % leaves) ^ (GROUP * parity)
    )

    note = ((8, 2 * rank), f32)
    dma = pltpu.SemaphoreType.DMA

    top_other = swapped(top_transfer, "leaf", 1)
    low, piece, gram, inverse = call(
        leaf_kernel,
        [(packed, bf16), ((leaves, *square), f32), (packed, f32), (packed, f32)],
        4.5,
        far=[bases, leaf_transfer],
        scratch=[pltpu.VMEM(bases.shape, f32), pltpu.VMEM(leaf_transfer.shape, f32), *work, dma((2,))],
    )
    gram_other = swapped(gram, "leaf", 1)
    halves, token = call(
        half_kernel,
        [((blocks, *square), bf16), note],
        2,
        scalars=[coupling_target],
        far=[jnp.transpose(couplings, (1, 2, 0))],
        arrays=[low],
        scratch=[pltpu.VMEM((rank, rank, blocks), bf16), turned, pltpu.VMEM((leaves, *square), bf16), dma((CHUNKS,))],
    )
    tables = gathered_by_xor(low, "leaf", leaf_bits)
    up, up_gram, middle_inverse = call(
        middle_kernel,
        [((GROUP, *square), f32), (packed, f32), (packed, f32)],
        4.5,
        scalars=[spot],
        arrays=[gram, gram_other, top_transfer, top_other, token],
        scratch=work,
    )
    up_other = swapped(up_gram, "leaf", 2)
    leaf_bases, leaf_transfers, token = call(
        leaf_output_kernel,
        [((share, *square), f32), ((leaves, *square), f32), note],
        2,
        scalars=[spot],
        far=[bases],
        arrays=[inverse, piece, middle_inverse],
        scratch=[pltpu.VMEM((share, *square), f32), dma],
    )
    top_low, top_inverse = call(
        top_kernel,
        [(packed, bf16), (packed, f32)],
        2.7,
        arrays=[up_gram, up_other, token],
        scratch=work,
    )
    top_tables = gathered_by_xor(top_low, "leaf", [bit + 2 for bit in quad_bits])
    new_couplings, top_transfers, top_halves, token = call(
        full_kernel,
        [((rank, rank, blocks), bf16), ((GROUP, *square), f32), ((top_blocks, *square), bf16), note],
        3.5,
        scalars=[source, top_left],
        far=[top_couplings],
        arrays=[halves, up, top_inverse, top_low, *tables],
        scratch=[
            pltpu.VMEM((rank, rank, blocks), bf16),
            turned,
            pltpu.VMEM((2 * sum(one.shape[0] for one in tables), *square), bf16),
            pltpu.VMEM(top_couplings.shape, bf16),
            pltpu.VMEM((leaves, *square), bf16),
            dma,
            dma((CHUNKS,)),
        ],
        far_outs=1,
    )
    (new_top_couplings,) = call(
        top_project_kernel,
        [((top_blocks, *square), bf16)],
        1.5,
        scalars=[top_right],
        arrays=[top_halves, token, *top_tables],
        scratch=[pltpu.VMEM((2 * sum(one.shape[0] for one in top_tables), *square), bf16)],
    )
    new_couplings = jnp.transpose(new_couplings, (2, 0, 1))
    return (leaf_bases, leaf_transfers, top_transfers, new_couplings, new_top_couplings)


def solution(mesh):
    in_specs = (
        P("leaf", None, None),
        P("leaf", None, None),
        P("leaf", None, None),
        P(("leaf", "near"), None, None),
        P(("leaf", "near")),
        P(("leaf", "near"), None),
        P(("leaf", "near")),
        P(("leaf", "near"), None, None),
        P(("leaf", "near")),
        P(("leaf", "near")),
    )
    out_specs = (
        P(("leaf", "near"), None, None),
        P("leaf", None, None),
        P("leaf", None, None),
        P(("leaf", "near"), None, None),
        P(("leaf", "near"), None, None),
    )
    return jax.shard_map(
        on_device, mesh=mesh, in_specs=in_specs, out_specs=out_specs, check_vma=False
    )
```

```python
import functools

import jax
import jax.numpy as jnp
from jax import lax
from jax.experimental import pallas as pl
from jax.experimental.pallas import tpu as pltpu
from jax.sharding import PartitionSpec as P

exact = lax.Precision.HIGHEST
f32 = jnp.float32
bf16 = jnp.bfloat16
BLOCK = 8
GROUP = 4
PITCH_EXTRA = 8
CHUNKS = 4
VMEM_LIMIT = 48 * 2**20
FLOPS = 1e9


def swapped(value, axis, mask):
    pairs = [(source, source ^ mask) for source in range(lax.axis_size(axis))]
    return lax.ppermute(value, axis, pairs)


def join_kernel(first, second, after, out):
    out[: first.shape[0]] = first[...]
    out[first.shape[0] :] = second[...]


def hold_kernel(value, after, out):
    out[...] = value[...]


def held(value, after):
    return call(hold_kernel, [(value.shape, value.dtype)], 0.1, arrays=[value, after])[0]


def joined_by_xor(value, axis, bits, after):
    for bit in bits:
        other = swapped(value, axis, 1 << bit)
        shape = (2 * value.shape[0], *value.shape[1:])
        (value,) = call(join_kernel, [(shape, value.dtype)], 0.2, arrays=[value, other, after])
    return value


def place_of(difference, bits):
    place = jnp.zeros_like(difference)
    for order, bit in enumerate(bits):
        place = place | (((difference >> bit) & 1) << order)
    return place


def dot_nn(a, b):
    return jnp.dot(a, b, precision=exact, preferred_element_type=f32)


def dot_tn(a, b):
    return lax.dot_general(a, b, (((0,), (0,)), ((), ())), precision=exact, preferred_element_type=f32)


def dot_nt(a, b):
    return lax.dot_general(a, b, (((1,), (1,)), ((), ())), precision=exact, preferred_element_type=f32)


def low_nn(a, b):
    return jnp.dot(a, b, preferred_element_type=f32)


def low_nt(a, b):
    return lax.dot_general(a, b, (((1,), (1,)), ((), ())), preferred_element_type=f32)


def eliminate(work, factor, inverse):
    rank = work.shape[1] // 2
    shape = (2 * GROUP, 2 * rank)
    lanes = lax.broadcasted_iota(jnp.int32, shape, 1)
    odd = lax.broadcasted_iota(jnp.int32, shape, 0) // GROUP
    upper = odd == 0
    column = lanes % rank
    side = lanes - column

    def pick(rows, index):
        return jnp.take_along_axis(rows, index, axis=1)

    def span(pair):
        return pl.ds(2 * GROUP * pair, 2 * GROUP)

    for start in range(0, rank, BLOCK):
        inside = (column >= start) & (column < start + BLOCK)
        rows = []
        for pair in range(start // 2, (start + BLOCK) // 2):
            both = work[span(pair), :]
            turned = pltpu.roll(both, GROUP, axis=0)
            rows += [jnp.where(upper, both, turned), jnp.where(upper, turned, both)]
        done = [(column == start + a).astype(f32) for a in range(BLOCK)]
        entry = [[pick(rows[a], side + (start + b)) if b >= a else None for b in range(BLOCK)] for a in range(BLOCK)]
        scaled = []
        for a in range(BLOCK):
            pivot = pltpu.reciprocal(entry[a][a], approx=True)
            scaled.append(rows[a] * pivot)
            for b in range(a + 1, BLOCK):
                share = entry[a][b] * pivot
                for c in range(b, BLOCK):
                    entry[b][c] = entry[b][c] - share * entry[a][c]
                rows[b] = rows[b] - share * rows[a]
                done[b] = done[b] - share * done[a]
        mixed = [jnp.where(inside, done[a], rows[a]) for a in range(BLOCK)]
        for pair in range((start + BLOCK) // 2, rank // 2):
            total = jnp.where(inside, 0.0, work[span(pair), :])
            index = side + odd + 2 * pair
            for a in range(BLOCK):
                total = total - pick(scaled[a], index) * mixed[a]
            work[span(pair), :] = total
        for a in range(0, BLOCK, 2):
            pair = (start + a) // 2
            row = odd + 2 * pair
            scale = lax.rsqrt(jnp.where(upper, entry[a][a], entry[a + 1][a + 1]))
            factor[span(pair), :] = jnp.where(
                column >= row, jnp.where(upper, rows[a], rows[a + 1]) * scale, 0.0
            )
            inverse[span(pair), :] = jnp.where(
                column <= row, jnp.where(upper, mixed[a], mixed[a + 1]) * scale, 0.0
            )


def matrix_pair(work, group):
    return pl.ds(group, work.shape[1] // 2, stride=GROUP)


def side_by_side(left, right):
    return jnp.concatenate([left, right], axis=1)


def gram_kernel(bases, gram):
    for g in range(GROUP):
        left, right = bases[g], bases[g + GROUP]
        gram[g] = side_by_side(dot_tn(left, left), dot_tn(right, right))


def congruent(gram, left, right):
    rank = gram.shape[0]
    first = dot_tn(left, dot_nn(gram[:, :rank], left))
    second = dot_tn(right, dot_nn(gram[:, rank:], right))
    return side_by_side(first, second)


def child_kernel(gram, transfer, top, message, token):
    token[...] = jnp.zeros_like(token)
    for g in range(GROUP):
        message[g] = congruent(gram[g], transfer[g], transfer[g + GROUP])
    for n in range(GROUP // 2):
        message[GROUP + n] = side_by_side(top[2 * n], top[2 * n + 1])


def middle_kernel(spot, mine, other, after, middle_gram, top_gram, token):
    rank = middle_gram.shape[1]
    token[...] = jnp.zeros_like(token)
    for g in range(GROUP):
        both = mine[g] + other[g]
        middle_gram[g] = both
        both = jnp.where(spot[1] == 0, both, pltpu.roll(both, rank, axis=1))
        lanes = slice(g % 2 * rank, (g % 2 + 1) * rank)
        top_gram[g] = congruent(both, mine[GROUP + g // 2][:, lanes], other[GROUP + g // 2][:, lanes])


def factor_kernel(terms, has_factor, has_low, *refs):
    grams, refs = refs[:terms], refs[terms + 1 :]
    outs, (work, factor, inverse) = refs[:-3], refs[-3:]
    for g in range(GROUP):
        work[matrix_pair(work, g), :] = grams[0][g] if terms == 1 else grams[0][g] + grams[1][g]
    eliminate(work, factor, inverse)
    for g in range(GROUP):
        both = factor[matrix_pair(work, g), :]
        outs[0][g] = inverse[matrix_pair(work, g), :]
        if has_factor:
            outs[1][g] = both
        if has_low:
            outs[-1][g] = both.astype(bf16)


def half_kernel(target, couplings_far, low, halves, token, couplings, turned, table, arrived):
    rank, _, count = couplings.shape
    pitch = turned.shape[0] // rank
    token[...] = jnp.zeros_like(token)
    chunk = rank // CHUNKS
    copies = []
    for k in range(CHUNKS):
        part = pl.ds(k * chunk, chunk)
        copies.append(pltpu.make_async_copy(couplings_far.at[part], couplings.at[part], arrived.at[k]))
        copies[k].start()
    for g in range(GROUP):
        both = low[g]
        table[g] = both[:, :rank]
        table[g + GROUP] = both[:, rank:]
    for k in range(CHUNKS):
        copies[k].wait()
        for m in range(k * chunk, (k + 1) * chunk):
            turned[m * pitch : m * pitch + count, :] = couplings[m].astype(f32).T
    for r in range(count):
        block = turned[pl.ds(r, rank, stride=pitch), :].astype(bf16)
        halves[r] = low_nn(table[target[r]], block).astype(bf16)


def output_kernel(
    spot,
    bases_far,
    after,
    leaf_factor,
    leaf_inverse,
    leaf_transfer,
    middle_factor,
    middle_inverse,
    top_transfer,
    top_inverse,
    leaf_bases,
    leaf_transfers,
    top_transfers,
    token,
    bases,
    arrived,
):
    share, _, rank = bases.shape
    token[...] = jnp.zeros_like(token)
    copy = pltpu.make_async_copy(bases_far.at[pl.ds(spot[0] * share, share)], bases, arrived)
    copy.start()
    for g in range(GROUP):
        for place, lanes in ((g, slice(0, rank)), (g + GROUP, slice(rank, 2 * rank))):
            piece = dot_nn(leaf_factor[g][:, lanes], leaf_transfer[place])
            leaf_transfers[place] = dot_nt(piece, middle_inverse[g][:, lanes])
        both = middle_factor[g]
        piece = dot_nn(jnp.where(spot[1] == 0, both[:, :rank], both[:, rank:]), top_transfer[g])
        top_transfers[g] = dot_nt(piece, top_inverse[g][:, :rank])
    copy.wait()
    for k in range(share):
        place = spot[0] * share + k
        both = leaf_inverse[place % GROUP]
        both = jnp.where(place < GROUP, both[:, :rank], both[:, rank:])
        leaf_bases[k] = dot_nt(bases[k], both)


def unpack(packed, table, base):
    count, rank = packed.shape[0], table.shape[2]

    def step(n, carry):
        both = packed[n]
        place = base + 2 * GROUP * (n // GROUP) + n % GROUP
        table[place] = both[:, :rank]
        table[place + GROUP] = both[:, rank:]
        return carry

    lax.fori_loop(0, count, step, 0, unroll=min(count, 16))


def unpack_all(packed, table):
    base = 0
    for one in packed:
        unpack(one, table, base)
        base += 2 * one.shape[0]


def full_kernel(source, halves, token, *rest):
    packed, (out_far, out, turned, table, left) = rest[:-5], rest[-5:]
    count, rank, _ = halves.shape
    pitch = turned.shape[0] // rank
    unpack_all(packed, table)
    for r in range(count):
        turned[pl.ds(r, rank, stride=pitch), :] = low_nt(halves[r], table[source[r]])
    chunk = rank // CHUNKS
    copies = []
    for k in range(CHUNKS):
        for m in range(k * chunk, (k + 1) * chunk):
            out[m] = turned[m * pitch : m * pitch + count, :].T.astype(bf16)
        part = pl.ds(k * chunk, chunk)
        copies.append(pltpu.make_async_copy(out.at[part], out_far.at[part], left.at[k]))
        copies[k].start()
    for copy in copies:
        copy.wait()


def top_project_kernel(target, source, couplings, after, *rest):
    packed, (out, token, table) = rest[:-3], rest[-3:]
    token[...] = jnp.zeros_like(token)
    unpack_all(packed, table)
    for r in range(couplings.shape[0]):
        half = low_nn(table[target[r]], couplings[r]).astype(bf16)
        out[r] = low_nt(half, table[source[r]]).astype(bf16)


vmem = pl.BlockSpec(memory_space=pltpu.VMEM)
smem = pl.BlockSpec(memory_space=pltpu.SMEM)
hbm = pl.BlockSpec(memory_space=pltpu.HBM)


def call(kernel, outs, microseconds, scalars=(), far=(), arrays=(), scratch=(), far_outs=0):
    return pl.pallas_call(
        kernel,
        out_shape=[jax.ShapeDtypeStruct(shape, dtype) for shape, dtype in outs],
        in_specs=[smem] * len(scalars) + [hbm] * len(far) + [vmem] * len(arrays),
        out_specs=[hbm] * far_outs + [vmem] * (len(outs) - far_outs),
        scratch_shapes=list(scratch),
        compiler_params=pltpu.CompilerParams(vmem_limit_bytes=VMEM_LIMIT),
        cost_estimate=pl.CostEstimate(flops=int(microseconds * FLOPS), bytes_accessed=0, transcendentals=0),
    )(*scalars, *far, *arrays)


def on_device(
    bases,
    leaf_transfer,
    top_transfer,
    couplings,
    coupling_target,
    coupling_dest,
    coupling_local,
    top_couplings,
    top_target,
    top_source,
):
    leaves, _, rank = bases.shape
    share = leaves // lax.axis_size("near")
    blocks, top_blocks = couplings.shape[0], top_couplings.shape[0]
    leaf_bits = list(range(lax.axis_size("leaf").bit_length() - 1))[::-1]
    quad_bits = [bit - 2 for bit in leaf_bits if bit >= 2]
    near_place, leaf_place = lax.axis_index("near"), lax.axis_index("leaf")
    parity = leaf_place % 2
    spot = jnp.stack([near_place, parity]).astype(jnp.int32)
    square = (rank, rank)
    packed = (GROUP, rank, 2 * rank)
    work = [pltpu.VMEM((rank * GROUP, 2 * rank), f32)] * 3
    turned = pltpu.VMEM((rank * (blocks + PITCH_EXTRA), rank), f32)

    source = place_of(coupling_dest[:, 0] ^ leaf_place, leaf_bits) * leaves + coupling_local
    top_left = top_target ^ (GROUP * parity)
    top_right = place_of((top_source // leaves) ^ (leaf_place // 4), quad_bits) * leaves + (
        (top_source % leaves) ^ (GROUP * parity)
    )

    note = ((8, 2 * rank), f32)
    dma = pltpu.SemaphoreType.DMA


    def factored(grams, after, has_factor, has_low):
        return call(
            functools.partial(factor_kernel, len(grams), has_factor, has_low),
            [(packed, f32)] * (1 + has_factor) + [(packed, bf16)] * has_low,
            2.6,
            arrays=[*grams, after],
            scratch=work,
        )

    (gram,) = call(gram_kernel, [(packed, f32)], 0.6, arrays=[bases])
    message, token = call(
        child_kernel,
        [((GROUP + GROUP // 2, *packed[1:]), f32), note],
        0.8,
        arrays=[gram, leaf_transfer, top_transfer],
    )
    message_other = swapped(message, "leaf", 1)
    leaf_inverse, leaf_factor, low = factored([gram], token, True, True)
    halves, half_token = call(
        half_kernel,
        [((blocks, *square), bf16), note],
        2.7,
        scalars=[coupling_target],
        far=[jnp.transpose(couplings, (1, 2, 0))],
        arrays=[low],
        scratch=[pltpu.VMEM((rank, rank, blocks), bf16), turned, pltpu.VMEM((leaves, *square), bf16), dma((CHUNKS,))],
    )
    middle_gram, top_gram, token = call(
        middle_kernel,
        [(packed, f32), (packed, f32), note],
        1.4,
        scalars=[spot],
        arrays=[message, message_other, half_token],
    )
    top_gram_other = swapped(top_gram, "leaf", 2)
    middle_inverse, middle_factor = factored([middle_gram], token, True, False)
    table = joined_by_xor(held(low, half_token), "leaf", leaf_bits[:1], middle_inverse)
    top_inverse, top_low = factored([top_gram, top_gram_other], table, False, True)
    top_table = joined_by_xor(top_low, "leaf", [bit + 2 for bit in quad_bits[:-1]], top_inverse)
    top_tables = [top_table, swapped(top_table, "leaf", 4 << quad_bits[-1])]
    table = joined_by_xor(table, "leaf", leaf_bits[1:-1], top_inverse)
    tables = [table, swapped(table, "leaf", 1 << leaf_bits[-1])]
    leaf_bases, leaf_transfers, top_transfers, token = call(
        output_kernel,
        [((share, *square), f32), ((leaves, *square), f32), ((GROUP, *square), f32), note],
        2.4,
        scalars=[spot],
        far=[bases],
        arrays=[
            table,
            leaf_factor,
            leaf_inverse,
            leaf_transfer,
            middle_factor,
            middle_inverse,
            top_transfer,
            top_inverse,
        ],
        scratch=[pltpu.VMEM((share, *square), f32), dma],
    )
    new_top_couplings, token = call(
        top_project_kernel,
        [((top_blocks, *square), bf16), note],
        1.5,
        scalars=[top_left, top_right],
        arrays=[top_couplings, token, *top_tables],
        scratch=[pltpu.VMEM((2 * sum(one.shape[0] for one in top_tables), *square), bf16)],
    )
    (new_couplings,) = call(
        full_kernel,
        [((rank, rank, blocks), bf16)],
        3.5,
        scalars=[source],
        arrays=[halves, token, *tables],
        scratch=[
            pltpu.VMEM((rank, rank, blocks), bf16),
            turned,
            pltpu.VMEM((2 * sum(one.shape[0] for one in tables), *square), bf16),
            dma((CHUNKS,)),
        ],
        far_outs=1,
    )
    new_couplings = jnp.transpose(new_couplings, (2, 0, 1))
    return (leaf_bases, leaf_transfers, top_transfers, new_couplings, new_top_couplings)


def solution(mesh):
    in_specs = (
        P("leaf", None, None),
        P("leaf", None, None),
        P("leaf", None, None),
        P(("leaf", "near"), None, None),
        P(("leaf", "near")),
        P(("leaf", "near"), None),
        P(("leaf", "near")),
        P(("leaf", "near"), None, None),
        P(("leaf", "near")),
        P(("leaf", "near")),
    )
    out_specs = (
        P(("leaf", "near"), None, None),
        P("leaf", None, None),
        P("leaf", None, None),
        P(("leaf", "near"), None, None),
        P(("leaf", "near"), None, None),
    )
    return jax.shard_map(
        on_device, mesh=mesh, in_specs=in_specs, out_specs=out_specs, check_vma=False
    )
```

```python
import functools

import jax
import jax.numpy as jnp
from jax import lax
from jax.experimental import pallas as pl
from jax.experimental.pallas import tpu as pltpu
from jax.sharding import PartitionSpec as P

exact = lax.Precision.HIGHEST
f32 = jnp.float32
bf16 = jnp.bfloat16
BLOCK = 8
GROUP = 4
PITCH_EXTRA = 8
CHUNKS = 4
VMEM_LIMIT = 48 * 2**20
FLOPS = 1e9


def swapped(value, axis, mask):
    pairs = [(source, source ^ mask) for source in range(lax.axis_size(axis))]
    return lax.ppermute(value, axis, pairs)


def join_kernel(first, second, after, out):
    out[: first.shape[0]] = first[...]
    out[first.shape[0] :] = second[...]


def hold_kernel(value, after, out):
    out[...] = value[...]


def held(value, after):
    return call(hold_kernel, [(value.shape, value.dtype)], 0.1, arrays=[value, after])[0]


def joined_by_xor(value, axis, bits, after):
    for bit in bits:
        other = swapped(value, axis, 1 << bit)
        shape = (2 * value.shape[0], *value.shape[1:])
        (value,) = call(join_kernel, [(shape, value.dtype)], 0.2, arrays=[value, other, after])
    return value


def place_of(difference, bits):
    place = jnp.zeros_like(difference)
    for order, bit in enumerate(bits):
        place = place | (((difference >> bit) & 1) << order)
    return place


def dot_nn(a, b):
    return jnp.dot(a, b, precision=exact, preferred_element_type=f32)


def dot_tn(a, b):
    return lax.dot_general(a, b, (((0,), (0,)), ((), ())), precision=exact, preferred_element_type=f32)


def dot_nt(a, b):
    return lax.dot_general(a, b, (((1,), (1,)), ((), ())), precision=exact, preferred_element_type=f32)


def low_nn(a, b):
    return jnp.dot(a, b, preferred_element_type=f32)


def low_nt(a, b):
    return lax.dot_general(a, b, (((1,), (1,)), ((), ())), preferred_element_type=f32)


def eliminate(work, factor, inverse):
    rank = work.shape[1] // 2
    middle = rank // 2
    shape = (2 * GROUP, 2 * rank)
    lanes = lax.broadcasted_iota(jnp.int32, shape, 1)
    odd = lax.broadcasted_iota(jnp.int32, shape, 0) // GROUP
    upper = odd == 0
    column = lanes % rank
    side = lanes - column

    def pick(rows, index):
        return jnp.take_along_axis(rows, index, axis=1)

    def span(pair):
        return pl.ds(2 * GROUP * pair, 2 * GROUP)

    for start in range(0, rank, BLOCK):
        inside = (column >= start) & (column < start + BLOCK)
        rows = []
        for pair in range(start // 2, (start + BLOCK) // 2):
            both = work[span(pair), :]
            turned = pltpu.roll(both, GROUP, axis=0)
            rows += [jnp.where(upper, both, turned), jnp.where(upper, turned, both)]
        done = [(column == start + a).astype(f32) for a in range(BLOCK)]
        entry = [[pick(rows[a], side + (start + b)) if b >= a else None for b in range(BLOCK)] for a in range(BLOCK)]
        scaled = []
        for a in range(BLOCK):
            pivot = pltpu.reciprocal(entry[a][a], approx=True)
            scaled.append(rows[a] * pivot)
            for b in range(a + 1, BLOCK):
                share = entry[a][b] * pivot
                for c in range(b, BLOCK):
                    entry[b][c] = entry[b][c] - share * entry[a][c]
                rows[b] = rows[b] - share * rows[a]
                done[b] = done[b] - share * done[a]
        mixed = [jnp.where(inside, done[a], rows[a]) for a in range(BLOCK)]
        for pair in range((start + BLOCK) // 2, (middle if start < middle else rank) // 2):
            total = jnp.where(inside, 0.0, work[span(pair), :])
            index = side + odd + 2 * pair
            for a in range(BLOCK):
                total = total - pick(scaled[a], index) * mixed[a]
            work[span(pair), :] = total
        for a in range(0, BLOCK, 2):
            pair = (start + a) // 2
            row = odd + 2 * pair
            scale = lax.rsqrt(jnp.where(upper, entry[a][a], entry[a + 1][a + 1]))
            factor[span(pair), :] = jnp.where(
                column >= row, jnp.where(upper, rows[a], rows[a + 1]) * scale, 0.0
            )
            inverse[span(pair), :] = jnp.where(
                column <= row, jnp.where(upper, mixed[a], mixed[a + 1]) * scale, 0.0
            )
        if start + BLOCK == middle:
            update_second_half(work, factor, inverse)


def update_second_half(work, factor, inverse):
    rank = work.shape[1] // 2
    middle = rank // 2
    shape = (middle, 2 * rank)
    lanes = lax.broadcasted_iota(jnp.int32, shape, 1)
    early = lanes % rank < middle
    for g in range(GROUP):
        above = pl.ds(g, middle, stride=GROUP)
        below = pl.ds(GROUP * middle + g, middle, stride=GROUP)
        rows = jnp.where(early, inverse[above, :], factor[above, :])
        product = dot_tn(rows, rows)
        taken = jnp.where(lanes < rank, product[middle:rank, :], product[rank + middle :, :])
        work[below, :] = jnp.where(early, 0.0, work[below, :]) - taken


def matrix_pair(work, group):
    return pl.ds(group, work.shape[1] // 2, stride=GROUP)


def side_by_side(left, right):
    return jnp.concatenate([left, right], axis=1)


def gram_kernel(bases, gram):
    for g in range(GROUP):
        left, right = bases[g], bases[g + GROUP]
        gram[g] = side_by_side(dot_tn(left, left), dot_tn(right, right))


def congruent(gram, left, right):
    rank = gram.shape[0]
    first = dot_tn(left, dot_nn(gram[:, :rank], left))
    second = dot_tn(right, dot_nn(gram[:, rank:], right))
    return side_by_side(first, second)


def child_kernel(gram, transfer, top, message, token):
    token[...] = jnp.zeros_like(token)
    for g in range(GROUP):
        message[g] = congruent(gram[g], transfer[g], transfer[g + GROUP])
    for n in range(GROUP // 2):
        message[GROUP + n] = side_by_side(top[2 * n], top[2 * n + 1])


def middle_kernel(spot, mine, other, after, middle_gram, top_gram, token):
    rank = middle_gram.shape[1]
    token[...] = jnp.zeros_like(token)
    first = spot[1] == 0
    for g in range(GROUP):
        lanes = slice(g % 2 * rank, (g % 2 + 1) * rank)
        own, sibling = mine[GROUP + g // 2][:, lanes], other[GROUP + g // 2][:, lanes]
        both = mine[g] + other[g]
        middle_gram[g] = both
        top_gram[g] = congruent(both, jnp.where(first, own, sibling), jnp.where(first, sibling, own))


def factor_kernel(terms, has_factor, has_low, *refs):
    grams, refs = refs[:terms], refs[terms + 1 :]
    outs, (work, factor, inverse) = refs[:-3], refs[-3:]
    for g in range(GROUP):
        work[matrix_pair(work, g), :] = grams[0][g] if terms == 1 else grams[0][g] + grams[1][g]
    eliminate(work, factor, inverse)
    for g in range(GROUP):
        both = factor[matrix_pair(work, g), :]
        outs[0][g] = inverse[matrix_pair(work, g), :]
        if has_factor:
            outs[1][g] = both
        if has_low:
            outs[-1][g] = both.astype(bf16)


def half_kernel(target, couplings, low, halves, token, turned, table):
    rank, _, count = couplings.shape
    pitch = turned.shape[0] // rank
    token[...] = jnp.zeros_like(token)
    for g in range(GROUP):
        both = low[g]
        table[g] = both[:, :rank]
        table[g + GROUP] = both[:, rank:]
    for m in range(rank):
        turned[m * pitch : m * pitch + count, :] = couplings[m].astype(f32).T
    for r in range(count):
        block = turned[pl.ds(r, rank, stride=pitch), :].astype(bf16)
        halves[r] = low_nn(table[target[r]], block).astype(bf16)


def output_kernel(
    spot,
    bases,
    after,
    leaf_factor,
    leaf_inverse,
    leaf_transfer,
    middle_factor,
    middle_inverse,
    top_transfer,
    top_inverse,
    leaf_bases,
    leaf_transfers,
    top_transfers,
    token,
):
    rank = bases.shape[2]
    share = leaf_bases.shape[0]
    token[...] = jnp.zeros_like(token)
    for n, lanes in enumerate((slice(0, rank), slice(rank, 2 * rank))):
        for g in range(GROUP):
            place = n * GROUP + g
            piece = dot_nn(leaf_factor[g][:, lanes], leaf_transfer[place])
            leaf_transfers[place] = dot_nt(piece, middle_inverse[g][:, lanes])
    for g in range(GROUP):
        left, right = (jnp.where(spot[1] == 0, both[:, :rank], both[:, rank:]) for both in (middle_factor[g], top_inverse[g]))
        top_transfers[g] = dot_nt(dot_nn(left, top_transfer[g]), right)
    for k in range(share):
        place = spot[0] * share + k
        both = leaf_inverse[place % GROUP]
        both = jnp.where(place < GROUP, both[:, :rank], both[:, rank:])
        leaf_bases[k] = dot_nt(bases[place], both)


def shares(count, steps):
    edges = [count * k // steps for k in range(steps + 1)]
    return [range(low, high) for low, high in zip(edges[:-1], edges[1:])]


def unpack(packed, table, base, turn):
    count, rank = packed.shape[0], table.shape[2]

    def step(n, carry):
        both = packed[n]
        place = base + 2 * GROUP * (n // GROUP) + n % GROUP
        if turn:
            both = both.T
            table[place] = both[:rank]
            table[place + GROUP] = both[rank:]
        else:
            table[place] = both[:, :rank]
            table[place + GROUP] = both[:, rank:]
        return carry

    lax.fori_loop(0, count, step, 0, unroll=min(count, 16))


def unpack_all(packed, table, turn):
    base = 0
    for one in packed:
        unpack(one, table, base, turn)
        base += 2 * one.shape[0]


def full_kernel(ready, source, halves, *rest):
    near, rest = rest[:ready], rest[ready:]
    far, rest = rest[-5 - ready : -5], rest[: -5 - ready] + rest[-5:]
    packed, (out_far, out, turned, table, left) = rest[:-5], rest[-5:]
    count, rank, _ = halves.shape
    pitch = turned.shape[0] // rank
    copies = [pltpu.make_async_copy(near[n], far[n], left.at[n]) for n in range(ready)]
    for copy in copies:
        copy.start()
    unpack_all(packed, table, True)
    for r in range(count):
        turned[pl.ds(r, rank, stride=pitch), :] = low_nn(halves[r], table[source[r]])
    for k, part in enumerate(shares(rank, CHUNKS)):
        for m in part:
            out[m] = turned[m * pitch : m * pitch + count, :].T.astype(bf16)
        place = pl.ds(part.start, len(part))
        copies.append(pltpu.make_async_copy(out.at[place], out_far.at[place], left.at[ready + k]))
        copies[-1].start()
    for copy in copies:
        copy.wait()


def top_project_kernel(target, source, couplings, after, *rest):
    packed, (out, table) = rest[:-2], rest[-2:]
    unpack_all(packed, table, False)
    for r in range(couplings.shape[0]):
        half = low_nn(table[target[r]], couplings[r]).astype(bf16)
        out[r] = low_nt(half, table[source[r]]).astype(bf16)


vmem = pl.BlockSpec(memory_space=pltpu.VMEM)
smem = pl.BlockSpec(memory_space=pltpu.SMEM)
hbm = pl.BlockSpec(memory_space=pltpu.HBM)


def call(kernel, outs, microseconds, scalars=(), far=(), arrays=(), scratch=(), far_outs=0):
    return pl.pallas_call(
        kernel,
        out_shape=[jax.ShapeDtypeStruct(shape, dtype) for shape, dtype in outs],
        in_specs=[smem] * len(scalars) + [hbm] * len(far) + [vmem] * len(arrays),
        out_specs=[hbm] * far_outs + [vmem] * (len(outs) - far_outs),
        scratch_shapes=list(scratch),
        compiler_params=pltpu.CompilerParams(vmem_limit_bytes=VMEM_LIMIT),
        cost_estimate=pl.CostEstimate(flops=int(microseconds * FLOPS), bytes_accessed=0, transcendentals=0),
    )(*scalars, *far, *arrays)


def on_device(
    bases,
    leaf_transfer,
    top_transfer,
    couplings,
    coupling_target,
    coupling_dest,
    coupling_local,
    top_couplings,
    top_target,
    top_source,
):
    leaves, _, rank = bases.shape
    share = leaves // lax.axis_size("near")
    blocks, top_blocks = couplings.shape[0], top_couplings.shape[0]
    leaf_bits = list(range(lax.axis_size("leaf").bit_length() - 1))[::-1]
    quad_bits = [bit - 2 for bit in leaf_bits if bit >= 2]
    near_place, leaf_place = lax.axis_index("near"), lax.axis_index("leaf")
    parity = leaf_place % 2
    spot = jnp.stack([near_place, parity]).astype(jnp.int32)
    square = (rank, rank)
    packed = (GROUP, rank, 2 * rank)
    work = [pltpu.VMEM((rank * GROUP, 2 * rank), f32)] * 3
    turned = pltpu.VMEM((rank * (blocks + PITCH_EXTRA), rank), f32)

    source = place_of(coupling_dest[:, 0] ^ leaf_place, leaf_bits) * leaves + coupling_local
    top_right = place_of((top_source // leaves) ^ (leaf_place // 4), quad_bits) * leaves + top_source % leaves
    note = ((8, 2 * rank), f32)
    dma = pltpu.SemaphoreType.DMA


    def factored(grams, after, has_factor, has_low):
        return call(
            functools.partial(factor_kernel, len(grams), has_factor, has_low),
            [(packed, f32)] * (1 + has_factor) + [(packed, bf16)] * has_low,
            2.6,
            arrays=[*grams, after],
            scratch=work,
        )

    (gram,) = call(gram_kernel, [(packed, f32)], 1.0, arrays=[bases])
    message, token = call(
        child_kernel,
        [((GROUP + GROUP // 2, *packed[1:]), f32), note],
        0.8,
        arrays=[gram, leaf_transfer, top_transfer],
    )
    message_other = swapped(message, "leaf", 1)
    leaf_inverse, leaf_factor, low = factored([gram], token, True, True)
    halves, half_token = call(
        half_kernel,
        [((blocks, *square), bf16), note],
        2.7,
        scalars=[coupling_target],
        arrays=[jnp.transpose(couplings, (1, 2, 0)), low],
        scratch=[turned, pltpu.VMEM((leaves, *square), bf16)],
    )
    middle_gram, top_gram, token = call(
        middle_kernel,
        [(packed, f32), (packed, f32), note],
        1.4,
        scalars=[spot],
        arrays=[message, message_other, half_token],
    )
    top_gram_other = swapped(top_gram, "leaf", 2)
    middle_inverse, middle_factor = factored([middle_gram], token, True, False)
    table = joined_by_xor(held(low, half_token), "leaf", leaf_bits[:1], middle_inverse)
    top_inverse, top_low = factored([top_gram, top_gram_other], table, False, True)
    top_table = joined_by_xor(top_low, "leaf", [bit + 2 for bit in quad_bits[:-1]], top_inverse)
    top_tables = [top_table, swapped(top_table, "leaf", 4 << quad_bits[-1])]
    table = joined_by_xor(table, "leaf", leaf_bits[1:-1], top_inverse)
    tables = [table, swapped(table, "leaf", 1 << leaf_bits[-1])]
    leaf_bases, leaf_transfers, top_transfers, token = call(
        output_kernel,
        [((share, *square), f32), ((leaves, *square), f32), ((GROUP, *square), f32), note],
        2.4,
        scalars=[spot],
        arrays=[
            bases,
            table,
            leaf_factor,
            leaf_inverse,
            leaf_transfer,
            middle_factor,
            middle_inverse,
            top_transfer,
            top_inverse,
        ],
    )
    (new_top_couplings,) = call(
        top_project_kernel,
        [((top_blocks, *square), bf16)],
        1.5,
        scalars=[top_target, top_right],
        arrays=[top_couplings, token, *top_tables],
        scratch=[pltpu.VMEM((2 * sum(one.shape[0] for one in top_tables), *square), bf16)],
    )
    ready = [leaf_bases, leaf_transfers, top_transfers, new_top_couplings]
    leaf_bases, leaf_transfers, top_transfers, new_top_couplings, new_couplings = call(
        functools.partial(full_kernel, len(ready)),
        [(one.shape, one.dtype) for one in ready] + [((rank, rank, blocks), bf16)],
        3.5,
        scalars=[source],
        arrays=[halves, *ready, *tables],
        scratch=[
            pltpu.VMEM((rank, rank, blocks), bf16),
            turned,
            pltpu.VMEM((2 * sum(one.shape[0] for one in tables), *square), bf16),
            dma((len(ready) + CHUNKS,)),
        ],
        far_outs=len(ready) + 1,
    )
    new_couplings = jnp.transpose(new_couplings, (2, 0, 1))
    return (leaf_bases, leaf_transfers, top_transfers, new_couplings, new_top_couplings)


def solution(mesh):
    in_specs = (
        P("leaf", None, None),
        P("leaf", None, None),
        P("leaf", None, None),
        P(("leaf", "near"), None, None),
        P(("leaf", "near")),
        P(("leaf", "near"), None),
        P(("leaf", "near")),
        P(("leaf", "near"), None, None),
        P(("leaf", "near")),
        P(("leaf", "near")),
    )
    out_specs = (
        P(("leaf", "near"), None, None),
        P("leaf", None, None),
        P("leaf", None, None),
        P(("leaf", "near"), None, None),
        P(("leaf", "near"), None, None),
    )
    return jax.shard_map(
        on_device, mesh=mesh, in_specs=in_specs, out_specs=out_specs, check_vma=False
    )
```

```python
import functools

import jax
import jax.numpy as jnp
from jax import lax
from jax.experimental import pallas as pl
from jax.experimental.pallas import tpu as pltpu
from jax.sharding import PartitionSpec as P

exact = lax.Precision.HIGHEST
f32 = jnp.float32
bf16 = jnp.bfloat16
BLOCK = 8
GROUP = 4
PITCH_EXTRA = 8
CHUNKS = 4
VMEM_LIMIT = 48 * 2**20
FLOPS = 1e9


def swapped(value, axis, mask):
    pairs = [(source, source ^ mask) for source in range(lax.axis_size(axis))]
    return lax.ppermute(value, axis, pairs)


def join_kernel(first, second, after, out):
    out[: first.shape[0]] = first[...]
    out[first.shape[0] :] = second[...]


def hold_kernel(value, after, out):
    out[...] = value[...]


def held(value, after):
    return call(hold_kernel, [(value.shape, value.dtype)], 0.1, arrays=[value, after])[0]


def joined_by_xor(value, axis, bits, after):
    for bit in bits:
        other = swapped(value, axis, 1 << bit)
        shape = (2 * value.shape[0], *value.shape[1:])
        (value,) = call(join_kernel, [(shape, value.dtype)], 0.2, arrays=[value, other, after])
    return value


def place_of(difference, bits):
    place = jnp.zeros_like(difference)
    for order, bit in enumerate(bits):
        place = place | (((difference >> bit) & 1) << order)
    return place


def dot_nn(a, b):
    return jnp.dot(a, b, precision=exact, preferred_element_type=f32)


def dot_tn(a, b):
    return lax.dot_general(a, b, (((0,), (0,)), ((), ())), precision=exact, preferred_element_type=f32)


def dot_nt(a, b):
    return lax.dot_general(a, b, (((1,), (1,)), ((), ())), precision=exact, preferred_element_type=f32)


def low_nn(a, b):
    return jnp.dot(a, b, preferred_element_type=f32)


def low_nt(a, b):
    return lax.dot_general(a, b, (((1,), (1,)), ((), ())), preferred_element_type=f32)


def eliminate(work, factor, inverse):
    rank = work.shape[1] // 2
    middle = rank // 2
    shape = (2 * GROUP, 2 * rank)
    lanes = lax.broadcasted_iota(jnp.int32, shape, 1)
    odd = lax.broadcasted_iota(jnp.int32, shape, 0) // GROUP
    upper = odd == 0
    column = lanes % rank
    side = lanes - column

    def pick(rows, index):
        return jnp.take_along_axis(rows, index, axis=1)

    def span(pair):
        return pl.ds(2 * GROUP * pair, 2 * GROUP)

    for start in range(0, rank, BLOCK):
        inside = (column >= start) & (column < start + BLOCK)
        rows = []
        for pair in range(start // 2, (start + BLOCK) // 2):
            both = work[span(pair), :]
            turned = pltpu.roll(both, GROUP, axis=0)
            rows += [jnp.where(upper, both, turned), jnp.where(upper, turned, both)]
        done = [(column == start + a).astype(f32) for a in range(BLOCK)]
        entry = [[pick(rows[a], side + (start + b)) if b >= a else None for b in range(BLOCK)] for a in range(BLOCK)]
        scaled = []
        for a in range(BLOCK):
            pivot = pltpu.reciprocal(entry[a][a], approx=True)
            scaled.append(rows[a] * pivot)
            for b in range(a + 1, BLOCK):
                share = entry[a][b] * pivot
                for c in range(b, BLOCK):
                    entry[b][c] = entry[b][c] - share * entry[a][c]
                rows[b] = rows[b] - share * rows[a]
                done[b] = done[b] - share * done[a]
        mixed = [jnp.where(inside, done[a], rows[a]) for a in range(BLOCK)]
        for pair in range((start + BLOCK) // 2, (middle if start < middle else rank) // 2):
            total = jnp.where(inside, 0.0, work[span(pair), :])
            index = side + odd + 2 * pair
            for a in range(BLOCK):
                total = total - pick(scaled[a], index) * mixed[a]
            work[span(pair), :] = total
        for a in range(0, BLOCK, 2):
            pair = (start + a) // 2
            row = odd + 2 * pair
            scale = lax.rsqrt(jnp.where(upper, entry[a][a], entry[a + 1][a + 1]))
            factor[span(pair), :] = jnp.where(
                column >= row, jnp.where(upper, rows[a], rows[a + 1]) * scale, 0.0
            )
            inverse[span(pair), :] = jnp.where(
                column <= row, jnp.where(upper, mixed[a], mixed[a + 1]) * scale, 0.0
            )
        if start + BLOCK == middle:
            update_second_half(work, factor, inverse)


def update_second_half(work, factor, inverse):
    rank = work.shape[1] // 2
    middle = rank // 2
    shape = (middle, 2 * rank)
    lanes = lax.broadcasted_iota(jnp.int32, shape, 1)
    early = lanes % rank < middle
    for g in range(GROUP):
        above = pl.ds(g, middle, stride=GROUP)
        below = pl.ds(GROUP * middle + g, middle, stride=GROUP)
        rows = jnp.where(early, inverse[above, :], factor[above, :])
        product = dot_tn(rows, rows)
        taken = jnp.where(lanes < rank, product[middle:rank, :], product[rank + middle :, :])
        work[below, :] = jnp.where(early, 0.0, work[below, :]) - taken


def matrix_pair(work, group):
    return pl.ds(group, work.shape[1] // 2, stride=GROUP)


def side_by_side(left, right):
    return jnp.concatenate([left, right], axis=1)


def pack_upper(pairs, out):
    rank = pairs[0].shape[0]
    half = rank // 2
    right = lax.broadcasted_iota(jnp.int32, (half, 2 * rank), 1) % rank >= half
    for n in range(GROUP // 2):
        first, second = pairs[2 * n], pairs[2 * n + 1]
        start = 3 * half * n
        out[start : start + half, :] = first[:half].astype(out.dtype)
        out[start + half : start + 2 * half, :] = second[:half].astype(out.dtype)
        turned = pltpu.roll(second[half:], 2 * rank - half, axis=1)
        out[start + 2 * half : start + 3 * half, :] = jnp.where(right, first[half:], turned).astype(out.dtype)


def unpack_upper(message):
    rank = message.shape[-1] // 2
    half = rank // 2
    right = lax.broadcasted_iota(jnp.int32, (half, 2 * rank), 1) % rank >= half
    pairs = []
    for n in range(GROUP // 2):
        start = 3 * half * n
        shared = message[start + 2 * half : start + 3 * half, :].astype(f32)
        for k, lower in enumerate((shared, pltpu.roll(shared, half, axis=1))):
            upper = message[start + k * half : start + (k + 1) * half, :]
            lower = jnp.where(right, lower, 0.0).astype(upper.dtype)
            pairs.append(jnp.concatenate([upper, lower], axis=0))
    return pairs


def gram_kernel(bases, gram):
    for g in range(GROUP):
        left, right = bases[g], bases[g + GROUP]
        gram[g] = side_by_side(dot_tn(left, left), dot_tn(right, right))


def congruent(gram, left, right):
    rank = gram.shape[0]
    first = dot_tn(left, dot_nn(gram[:, :rank], left))
    second = dot_tn(right, dot_nn(gram[:, rank:], right))
    return side_by_side(first, second)


def child_kernel(gram, transfer, top, message, token):
    token[...] = jnp.zeros_like(token)
    for g in range(GROUP):
        message[g] = congruent(gram[g], transfer[g], transfer[g + GROUP])
    for n in range(GROUP // 2):
        message[GROUP + n] = side_by_side(top[2 * n], top[2 * n + 1])


def middle_kernel(spot, mine, other, after, middle_gram, top_gram, message, token):
    rank = middle_gram.shape[1]
    token[...] = jnp.zeros_like(token)
    first = spot[1] == 0
    grams = []
    for g in range(GROUP):
        lanes = slice(g % 2 * rank, (g % 2 + 1) * rank)
        own, sibling = mine[GROUP + g // 2][:, lanes], other[GROUP + g // 2][:, lanes]
        both = mine[g] + other[g]
        middle_gram[g] = both
        grams.append(congruent(both, jnp.where(first, own, sibling), jnp.where(first, sibling, own)))
        top_gram[g] = grams[g]
    pack_upper(grams, message)


def factor_kernel(terms, has_factor, has_low, *refs):
    grams, refs = refs[:terms], refs[terms + 1 :]
    outs, (work, factor, inverse) = refs[:-3], refs[-3:]
    more = unpack_upper(grams[1]) if terms == 2 else None
    for g in range(GROUP):
        work[matrix_pair(work, g), :] = grams[0][g] if more is None else grams[0][g] + more[g]
    eliminate(work, factor, inverse)
    pairs = [factor[matrix_pair(work, g), :] for g in range(GROUP)]
    if has_low:
        pack_upper(pairs, outs[-1].at[0])
    for g in range(GROUP):
        outs[0][g] = inverse[matrix_pair(work, g), :]
        if has_factor:
            outs[1][g] = pairs[g]


def half_kernel(target, couplings, low, halves, token, turned, table):
    rank, _, count = couplings.shape
    pitch = turned.shape[0] // rank
    token[...] = jnp.zeros_like(token)
    for g in range(GROUP):
        both = low[g].astype(bf16)
        table[g] = both[:, :rank]
        table[g + GROUP] = both[:, rank:]
    for m in range(rank):
        turned[m * pitch : m * pitch + count, :] = couplings[m].astype(f32).T
    for r in range(count):
        block = turned[pl.ds(r, rank, stride=pitch), :].astype(bf16)
        halves[r] = low_nn(table[target[r]], block).astype(bf16)


def output_kernel(
    spot,
    target,
    bases,
    after,
    top_couplings,
    top_low,
    leaf_factor,
    leaf_inverse,
    leaf_transfer,
    middle_factor,
    middle_inverse,
    top_transfer,
    top_inverse,
    leaf_bases,
    leaf_transfers,
    top_transfers,
    top_halves,
    table,
):
    rank = bases.shape[2]
    share = leaf_bases.shape[0]
    unpack(top_low, table, 0, False)
    for r in range(top_couplings.shape[0]):
        top_halves[r] = low_nn(table[target[r]], top_couplings[r]).astype(bf16)
    for n, lanes in enumerate((slice(0, rank), slice(rank, 2 * rank))):
        for g in range(GROUP):
            place = n * GROUP + g
            piece = dot_nn(leaf_factor[g][:, lanes], leaf_transfer[place])
            leaf_transfers[place] = dot_nt(piece, middle_inverse[g][:, lanes])
    for g in range(GROUP):
        left, right = (jnp.where(spot[1] == 0, both[:, :rank], both[:, rank:]) for both in (middle_factor[g], top_inverse[g]))
        top_transfers[g] = dot_nt(dot_nn(left, top_transfer[g]), right)
    for k in range(share):
        place = spot[0] * share + k
        both = leaf_inverse[place % GROUP]
        both = jnp.where(place < GROUP, both[:, :rank], both[:, rank:])
        leaf_bases[k] = dot_nt(bases[place], both)


def shares(count, steps):
    edges = [count * k // steps for k in range(steps + 1)]
    return [range(low, high) for low, high in zip(edges[:-1], edges[1:])]


def unpack(packed, table, base, turn):
    count, rank = packed.shape[0], table.shape[2]

    def step(n, carry):
        for g, both in enumerate(unpack_upper(packed.at[n])):
            place = base + 2 * GROUP * n + g
            if turn:
                both = both.T
                table[place] = both[:rank]
                table[place + GROUP] = both[rank:]
            else:
                table[place] = both[:, :rank]
                table[place + GROUP] = both[:, rank:]
        return carry

    lax.fori_loop(0, count, step, 0, unroll=min(count, 4))


def unpack_all(packed, table, turn):
    base = 0
    for one in packed:
        unpack(one, table, base, turn)
        base += 2 * GROUP * one.shape[0]


def full_kernel(ready, source, halves, *rest):
    near, rest = rest[:ready], rest[ready:]
    far, rest = rest[-5 - ready : -5], rest[: -5 - ready] + rest[-5:]
    packed, (out_far, out, turned, table, left) = rest[:-5], rest[-5:]
    count, rank, _ = halves.shape
    pitch = turned.shape[0] // rank
    copies = [pltpu.make_async_copy(near[n], far[n], left.at[n]) for n in range(ready)]
    for copy in copies:
        copy.start()
    unpack_all(packed, table, True)
    for r in range(count):
        turned[pl.ds(r, rank, stride=pitch), :] = low_nn(halves[r], table[source[r]])
    for k, part in enumerate(shares(rank, CHUNKS)):
        for m in part:
            out[m] = turned[m * pitch : m * pitch + count, :].T.astype(bf16)
        place = pl.ds(part.start, len(part))
        copies.append(pltpu.make_async_copy(out.at[place], out_far.at[place], left.at[ready + k]))
        copies[-1].start()
    for copy in copies:
        copy.wait()


def top_project_kernel(source, halves, *rest):
    packed, (out, table) = rest[:-2], rest[-2:]
    unpack_all(packed, table, False)
    for r in range(halves.shape[0]):
        out[r] = low_nt(halves[r], table[source[r]]).astype(bf16)


vmem = pl.BlockSpec(memory_space=pltpu.VMEM)
smem = pl.BlockSpec(memory_space=pltpu.SMEM)
hbm = pl.BlockSpec(memory_space=pltpu.HBM)


def call(kernel, outs, microseconds, scalars=(), far=(), arrays=(), scratch=(), far_outs=0):
    return pl.pallas_call(
        kernel,
        out_shape=[jax.ShapeDtypeStruct(shape, dtype) for shape, dtype in outs],
        in_specs=[smem] * len(scalars) + [hbm] * len(far) + [vmem] * len(arrays),
        out_specs=[hbm] * far_outs + [vmem] * (len(outs) - far_outs),
        scratch_shapes=list(scratch),
        compiler_params=pltpu.CompilerParams(vmem_limit_bytes=VMEM_LIMIT),
        cost_estimate=pl.CostEstimate(flops=int(microseconds * FLOPS), bytes_accessed=0, transcendentals=0),
    )(*scalars, *far, *arrays)


def on_device(
    bases,
    leaf_transfer,
    top_transfer,
    couplings,
    coupling_target,
    coupling_dest,
    coupling_local,
    top_couplings,
    top_target,
    top_source,
):
    leaves, _, rank = bases.shape
    share = leaves // lax.axis_size("near")
    blocks, top_blocks = couplings.shape[0], top_couplings.shape[0]
    leaf_bits = list(range(lax.axis_size("leaf").bit_length() - 1))[::-1]
    quad_bits = [bit - 2 for bit in leaf_bits if bit >= 2]
    near_place, leaf_place = lax.axis_index("near"), lax.axis_index("leaf")
    parity = leaf_place % 2
    spot = jnp.stack([near_place, parity]).astype(jnp.int32)
    square = (rank, rank)
    packed = (GROUP, rank, 2 * rank)
    work = [pltpu.VMEM((rank * GROUP, 2 * rank), f32)] * 3
    turned = pltpu.VMEM((rank * (blocks + PITCH_EXTRA), rank), f32)

    source = place_of(coupling_dest[:, 0] ^ leaf_place, leaf_bits) * leaves + coupling_local
    top_right = place_of((top_source // leaves) ^ (leaf_place // 4), quad_bits) * leaves + top_source % leaves
    note = ((8, 2 * rank), f32)
    dma = pltpu.SemaphoreType.DMA


    uppers = (GROUP // 2 * 3 * (rank // 2), 2 * rank)

    def factored(grams, after, has_factor, has_low):
        return call(
            functools.partial(factor_kernel, len(grams), has_factor, has_low),
            [(packed, f32)] * (1 + has_factor) + [((1, *uppers), bf16)] * has_low,
            2.6,
            arrays=[*grams, after],
            scratch=work,
        )

    (gram,) = call(gram_kernel, [(packed, f32)], 1.0, arrays=[bases])
    message, token = call(
        child_kernel,
        [((GROUP + GROUP // 2, *packed[1:]), f32), note],
        0.8,
        arrays=[gram, leaf_transfer, top_transfer],
    )
    message_other = swapped(message, "leaf", 1)
    leaf_inverse, leaf_factor, low = factored([gram], token, True, True)
    halves, half_token = call(
        half_kernel,
        [((blocks, *square), bf16), note],
        2.7,
        scalars=[coupling_target],
        arrays=[jnp.transpose(couplings, (1, 2, 0)), leaf_factor],
        scratch=[turned, pltpu.VMEM((leaves, *square), bf16)],
    )
    middle_gram, top_gram, top_message, token = call(
        middle_kernel,
        [(packed, f32), (packed, f32), (uppers, f32), note],
        1.4,
        scalars=[spot],
        arrays=[message, message_other, half_token],
    )
    top_gram_other = swapped(top_message, "leaf", 2)
    middle_inverse, middle_factor = factored([middle_gram], token, True, False)
    table = joined_by_xor(held(low, half_token), "leaf", leaf_bits[:-2], middle_inverse)
    tables = [table, swapped(table, "leaf", 1 << leaf_bits[-2])]
    tables += [swapped(one, "leaf", 1 << leaf_bits[-1]) for one in tables]
    top_inverse, top_low = factored([top_gram, top_gram_other], table, False, True)
    top_table = joined_by_xor(top_low, "leaf", [bit + 2 for bit in quad_bits[:-1]], top_inverse)
    top_tables = [top_table, swapped(top_table, "leaf", 4 << quad_bits[-1])]
    leaf_bases, leaf_transfers, top_transfers, top_halves = call(
        output_kernel,
        [((share, *square), f32), ((leaves, *square), f32), ((GROUP, *square), f32), ((top_blocks, *square), bf16)],
        2.5,
        scalars=[spot, top_target],
        arrays=[
            bases,
            tables[1],
            top_couplings,
            top_low,
            leaf_factor,
            leaf_inverse,
            leaf_transfer,
            middle_factor,
            middle_inverse,
            top_transfer,
            top_inverse,
        ],
        scratch=[pltpu.VMEM((leaves, *square), bf16)],
    )
    (new_top_couplings,) = call(
        top_project_kernel,
        [((top_blocks, *square), bf16)],
        1.3,
        scalars=[top_right],
        arrays=[top_halves, *top_tables],
        scratch=[pltpu.VMEM((leaves * sum(one.shape[0] for one in top_tables), *square), bf16)],
    )
    ready = [leaf_bases, leaf_transfers, top_transfers, new_top_couplings]
    leaf_bases, leaf_transfers, top_transfers, new_top_couplings, new_couplings = call(
        functools.partial(full_kernel, len(ready)),
        [(one.shape, one.dtype) for one in ready] + [((rank, rank, blocks), bf16)],
        3.5,
        scalars=[source],
        arrays=[halves, *ready, *tables],
        scratch=[
            pltpu.VMEM((rank, rank, blocks), bf16),
            turned,
            pltpu.VMEM((leaves * sum(one.shape[0] for one in tables), *square), bf16),
            dma((len(ready) + CHUNKS,)),
        ],
        far_outs=len(ready) + 1,
    )
    new_couplings = jnp.transpose(new_couplings, (2, 0, 1))
    return (leaf_bases, leaf_transfers, top_transfers, new_couplings, new_top_couplings)


def solution(mesh):
    in_specs = (
        P("leaf", None, None),
        P("leaf", None, None),
        P("leaf", None, None),
        P(("leaf", "near"), None, None),
        P(("leaf", "near")),
        P(("leaf", "near"), None),
        P(("leaf", "near")),
        P(("leaf", "near"), None, None),
        P(("leaf", "near")),
        P(("leaf", "near")),
    )
    out_specs = (
        P(("leaf", "near"), None, None),
        P("leaf", None, None),
        P("leaf", None, None),
        P(("leaf", "near"), None, None),
        P(("leaf", "near"), None, None),
    )
    return jax.shard_map(
        on_device, mesh=mesh, in_specs=in_specs, out_specs=out_specs, check_vma=False
    )
```

```python
import functools

import jax
import jax.numpy as jnp
from jax import lax
from jax.experimental import pallas as pl
from jax.experimental.pallas import tpu as pltpu
from jax.sharding import PartitionSpec as P

exact = lax.Precision.HIGHEST
f32 = jnp.float32
bf16 = jnp.bfloat16
BLOCK = 8
GROUP = 4
PITCH_EXTRA = 8
CHUNKS = 4
VMEM_LIMIT = 48 * 2**20
FLOPS = 1e9


def swapped(value, axis, mask):
    pairs = [(source, source ^ mask) for source in range(lax.axis_size(axis))]
    return lax.ppermute(value, axis, pairs)


def join_kernel(first, second, after, out):
    out[: first.shape[0]] = first[...]
    out[first.shape[0] :] = second[...]


def hold_kernel(value, after, out):
    out[...] = value[...]


def held(value, after):
    return call(hold_kernel, [(value.shape, value.dtype)], 0.1, arrays=[value, after])[0]


def joined_by_xor(value, axis, bits, after):
    for bit in bits:
        other = swapped(value, axis, 1 << bit)
        shape = (2 * value.shape[0], *value.shape[1:])
        (value,) = call(join_kernel, [(shape, value.dtype)], 0.2, arrays=[value, other, after])
    return value


def place_of(difference, bits):
    place = jnp.zeros_like(difference)
    for order, bit in enumerate(bits):
        place = place | (((difference >> bit) & 1) << order)
    return place


def dot_nn(a, b):
    return jnp.dot(a, b, precision=exact, preferred_element_type=f32)


def dot_tn(a, b):
    return lax.dot_general(a, b, (((0,), (0,)), ((), ())), precision=exact, preferred_element_type=f32)


def near_nn(a, b):
    return jnp.dot(a, b, precision=lax.Precision.HIGH, preferred_element_type=f32)


def near_nt(a, b):
    return lax.dot_general(
        a, b, (((1,), (1,)), ((), ())), precision=lax.Precision.HIGH, preferred_element_type=f32
    )


def low_nn(a, b):
    return jnp.dot(a, b, preferred_element_type=f32)


def low_nt(a, b):
    return lax.dot_general(a, b, (((1,), (1,)), ((), ())), preferred_element_type=f32)


def eliminate(work, factor, inverse):
    rank = work.shape[1] // 2
    middle = rank // 2
    shape = (2 * GROUP, 2 * rank)
    lanes = lax.broadcasted_iota(jnp.int32, shape, 1)
    odd = lax.broadcasted_iota(jnp.int32, shape, 0) // GROUP
    upper = odd == 0
    column = lanes % rank
    side = lanes - column

    def pick(rows, index):
        return jnp.take_along_axis(rows, index, axis=1)

    def span(pair):
        return pl.ds(2 * GROUP * pair, 2 * GROUP)

    for start in range(0, rank, BLOCK):
        inside = (column >= start) & (column < start + BLOCK)
        rows = []
        for pair in range(start // 2, (start + BLOCK) // 2):
            both = work[span(pair), :]
            turned = pltpu.roll(both, GROUP, axis=0)
            rows += [jnp.where(upper, both, turned), jnp.where(upper, turned, both)]
        done = [(column == start + a).astype(f32) for a in range(BLOCK)]
        entry = [[pick(rows[a], side + (start + b)) if b >= a else None for b in range(BLOCK)] for a in range(BLOCK)]
        scaled = []
        for a in range(BLOCK):
            pivot = pltpu.reciprocal(entry[a][a], approx=True)
            scaled.append(rows[a] * pivot)
            for b in range(a + 1, BLOCK):
                share = entry[a][b] * pivot
                for c in range(b, BLOCK):
                    entry[b][c] = entry[b][c] - share * entry[a][c]
                rows[b] = rows[b] - share * rows[a]
                done[b] = done[b] - share * done[a]
        mixed = [jnp.where(inside, done[a], rows[a]) for a in range(BLOCK)]
        for pair in range((start + BLOCK) // 2, (middle if start < middle else rank) // 2):
            total = jnp.where(inside, 0.0, work[span(pair), :])
            index = side + odd + 2 * pair
            for a in range(BLOCK):
                total = total - pick(scaled[a], index) * mixed[a]
            work[span(pair), :] = total
        for a in range(0, BLOCK, 2):
            pair = (start + a) // 2
            row = odd + 2 * pair
            scale = lax.rsqrt(jnp.where(upper, entry[a][a], entry[a + 1][a + 1]))
            factor[span(pair), :] = jnp.where(
                column >= row, jnp.where(upper, rows[a], rows[a + 1]) * scale, 0.0
            )
            inverse[span(pair), :] = jnp.where(
                column <= row, jnp.where(upper, mixed[a], mixed[a + 1]) * scale, 0.0
            )
        if start + BLOCK == middle:
            update_second_half(work, factor, inverse)


def update_second_half(work, factor, inverse):
    rank = work.shape[1] // 2
    middle = rank // 2
    shape = (middle, 2 * rank)
    lanes = lax.broadcasted_iota(jnp.int32, shape, 1)
    early = lanes % rank < middle
    for g in range(GROUP):
        above = pl.ds(g, middle, stride=GROUP)
        below = pl.ds(GROUP * middle + g, middle, stride=GROUP)
        rows = jnp.where(early, inverse[above, :], factor[above, :])
        product = dot_tn(rows, rows)
        taken = jnp.where(lanes < rank, product[middle:rank, :], product[rank + middle :, :])
        work[below, :] = jnp.where(early, 0.0, work[below, :]) - taken


def matrix_pair(work, group):
    return pl.ds(group, work.shape[1] // 2, stride=GROUP)


def side_by_side(left, right):
    return jnp.concatenate([left, right], axis=1)


def pack_upper(pairs, out):
    rank = pairs[0].shape[0]
    half = rank // 2
    right = lax.broadcasted_iota(jnp.int32, (half, 2 * rank), 1) % rank >= half
    for n in range(GROUP // 2):
        first, second = pairs[2 * n], pairs[2 * n + 1]
        start = 3 * half * n
        out[start : start + half, :] = first[:half].astype(out.dtype)
        out[start + half : start + 2 * half, :] = second[:half].astype(out.dtype)
        turned = pltpu.roll(second[half:], 2 * rank - half, axis=1)
        out[start + 2 * half : start + 3 * half, :] = jnp.where(right, first[half:], turned).astype(out.dtype)


def unpack_upper(message):
    rank = message.shape[-1] // 2
    half = rank // 2
    right = lax.broadcasted_iota(jnp.int32, (half, 2 * rank), 1) % rank >= half
    pairs = []
    for n in range(GROUP // 2):
        start = 3 * half * n
        shared = message[start + 2 * half : start + 3 * half, :].astype(f32)
        for k, lower in enumerate((shared, pltpu.roll(shared, half, axis=1))):
            upper = message[start + k * half : start + (k + 1) * half, :]
            lower = jnp.where(right, lower, 0.0).astype(upper.dtype)
            pairs.append(jnp.concatenate([upper, lower], axis=0))
    return pairs


def gram_kernel(bases, gram):
    for g in range(GROUP):
        left, right = bases[g], bases[g + GROUP]
        gram[g] = side_by_side(dot_tn(left, left), dot_tn(right, right))


def congruent(gram, left, right):
    rank = gram.shape[0]
    first = dot_tn(left, dot_nn(gram[:, :rank], left))
    second = dot_tn(right, dot_nn(gram[:, rank:], right))
    return side_by_side(first, second)


def child_kernel(gram, transfer, top, message, token):
    token[...] = jnp.zeros_like(token)
    for g in range(GROUP):
        message[g] = congruent(gram[g], transfer[g], transfer[g + GROUP])
    for n in range(GROUP // 2):
        message[GROUP + n] = side_by_side(top[2 * n], top[2 * n + 1])


def middle_kernel(spot, mine, other, after, middle_gram, top_gram, message, token):
    rank = middle_gram.shape[1]
    token[...] = jnp.zeros_like(token)
    first = spot[1] == 0
    grams = []
    for g in range(GROUP):
        lanes = slice(g % 2 * rank, (g % 2 + 1) * rank)
        own, sibling = mine[GROUP + g // 2][:, lanes], other[GROUP + g // 2][:, lanes]
        both = mine[g] + other[g]
        middle_gram[g] = both
        grams.append(congruent(both, jnp.where(first, own, sibling), jnp.where(first, sibling, own)))
        top_gram[g] = grams[g]
    pack_upper(grams, message)


def factor_kernel(terms, has_factor, has_low, *refs):
    grams, refs = refs[:terms], refs[terms + 1 :]
    outs, (work, factor, inverse) = refs[:-3], refs[-3:]
    more = unpack_upper(grams[1]) if terms == 2 else None
    for g in range(GROUP):
        work[matrix_pair(work, g), :] = grams[0][g] if more is None else grams[0][g] + more[g]
    eliminate(work, factor, inverse)
    pairs = [factor[matrix_pair(work, g), :] for g in range(GROUP)]
    if has_low:
        pack_upper(pairs, outs[-1].at[0])
    for g in range(GROUP):
        outs[0][g] = inverse[matrix_pair(work, g), :]
        if has_factor:
            outs[1][g] = pairs[g]


def half_kernel(target, couplings, low, halves, token, turned, table):
    rank, _, count = couplings.shape
    pitch = turned.shape[0] // rank
    token[...] = jnp.zeros_like(token)
    for g in range(GROUP):
        both = low[g].astype(bf16)
        table[g] = both[:, :rank]
        table[g + GROUP] = both[:, rank:]
    for m in range(rank):
        turned[m * pitch : m * pitch + count, :] = couplings[m].astype(f32).T
    for r in range(count):
        block = turned[pl.ds(r, rank, stride=pitch), :].astype(bf16)
        halves[r] = low_nn(table[target[r]], block).astype(bf16)


def output_kernel(
    spot,
    target,
    bases,
    after,
    top_couplings,
    top_low,
    leaf_factor,
    leaf_inverse,
    leaf_transfer,
    middle_factor,
    middle_inverse,
    top_transfer,
    top_inverse,
    leaf_bases,
    leaf_transfers,
    top_transfers,
    top_halves,
    table,
):
    rank = bases.shape[2]
    share = leaf_bases.shape[0]
    unpack(top_low, table, 0, False)
    for r in range(top_couplings.shape[0]):
        top_halves[r] = low_nn(table[target[r]], top_couplings[r]).astype(bf16)
    for n, lanes in enumerate((slice(0, rank), slice(rank, 2 * rank))):
        for g in range(GROUP):
            place = n * GROUP + g
            piece = near_nn(leaf_factor[g][:, lanes], leaf_transfer[place])
            leaf_transfers[place] = near_nt(piece, middle_inverse[g][:, lanes])
    for g in range(GROUP):
        left, right = (jnp.where(spot[1] == 0, both[:, :rank], both[:, rank:]) for both in (middle_factor[g], top_inverse[g]))
        top_transfers[g] = near_nt(near_nn(left, top_transfer[g]), right)
    for k in range(share):
        place = spot[0] * share + k
        both = leaf_inverse[place % GROUP]
        both = jnp.where(place < GROUP, both[:, :rank], both[:, rank:])
        leaf_bases[k] = near_nt(bases[place], both)


def shares(count, steps):
    edges = [count * k // steps for k in range(steps + 1)]
    return [range(low, high) for low, high in zip(edges[:-1], edges[1:])]


def unpack(packed, table, base, turn):
    count, rank = packed.shape[0], table.shape[2]

    def step(n, carry):
        for g, both in enumerate(unpack_upper(packed.at[n])):
            place = base + 2 * GROUP * n + g
            if turn:
                both = both.T
                table[place] = both[:rank]
                table[place + GROUP] = both[rank:]
            else:
                table[place] = both[:, :rank]
                table[place + GROUP] = both[:, rank:]
        return carry

    lax.fori_loop(0, count, step, 0, unroll=min(count, 4))


def unpack_all(packed, table, turn):
    base = 0
    for one in packed:
        unpack(one, table, base, turn)
        base += 2 * GROUP * one.shape[0]


def full_kernel(ready, source, halves, *rest):
    near, rest = rest[:ready], rest[ready:]
    far, rest = rest[-5 - ready : -5], rest[: -5 - ready] + rest[-5:]
    packed, (out_far, out, turned, table, left) = rest[:-5], rest[-5:]
    count, rank, _ = halves.shape
    pitch = turned.shape[0] // rank
    copies = [pltpu.make_async_copy(near[n], far[n], left.at[n]) for n in range(ready)]
    for copy in copies:
        copy.start()
    unpack_all(packed, table, True)
    for r in range(count):
        turned[pl.ds(r, rank, stride=pitch), :] = low_nn(halves[r], table[source[r]])
    for k, part in enumerate(shares(rank, CHUNKS)):
        for m in part:
            out[m] = turned[m * pitch : m * pitch + count, :].T.astype(bf16)
        place = pl.ds(part.start, len(part))
        copies.append(pltpu.make_async_copy(out.at[place], out_far.at[place], left.at[ready + k]))
        copies[-1].start()
    for copy in copies:
        copy.wait()


def top_project_kernel(source, halves, *rest):
    packed, (out, table) = rest[:-2], rest[-2:]
    unpack_all(packed, table, False)
    for r in range(halves.shape[0]):
        out[r] = low_nt(halves[r], table[source[r]]).astype(bf16)


vmem = pl.BlockSpec(memory_space=pltpu.VMEM)
smem = pl.BlockSpec(memory_space=pltpu.SMEM)
hbm = pl.BlockSpec(memory_space=pltpu.HBM)


def call(kernel, outs, microseconds, scalars=(), far=(), arrays=(), scratch=(), far_outs=0):
    return pl.pallas_call(
        kernel,
        out_shape=[jax.ShapeDtypeStruct(shape, dtype) for shape, dtype in outs],
        in_specs=[smem] * len(scalars) + [hbm] * len(far) + [vmem] * len(arrays),
        out_specs=[hbm] * far_outs + [vmem] * (len(outs) - far_outs),
        scratch_shapes=list(scratch),
        compiler_params=pltpu.CompilerParams(vmem_limit_bytes=VMEM_LIMIT),
        cost_estimate=pl.CostEstimate(flops=int(microseconds * FLOPS), bytes_accessed=0, transcendentals=0),
    )(*scalars, *far, *arrays)


def on_device(
    bases,
    leaf_transfer,
    top_transfer,
    couplings,
    coupling_target,
    coupling_dest,
    coupling_local,
    top_couplings,
    top_target,
    top_source,
):
    leaves, _, rank = bases.shape
    share = leaves // lax.axis_size("near")
    blocks, top_blocks = couplings.shape[0], top_couplings.shape[0]
    leaf_bits = list(range(lax.axis_size("leaf").bit_length() - 1))[::-1]
    quad_bits = [bit - 2 for bit in leaf_bits if bit >= 2]
    near_place, leaf_place = lax.axis_index("near"), lax.axis_index("leaf")
    parity = leaf_place % 2
    spot = jnp.stack([near_place, parity]).astype(jnp.int32)
    square = (rank, rank)
    packed = (GROUP, rank, 2 * rank)
    work = [pltpu.VMEM((rank * GROUP, 2 * rank), f32)] * 3
    turned = pltpu.VMEM((rank * (blocks + PITCH_EXTRA), rank), f32)

    source = place_of(coupling_dest[:, 0] ^ leaf_place, leaf_bits) * leaves + coupling_local
    top_right = place_of((top_source // leaves) ^ (leaf_place // 4), quad_bits) * leaves + top_source % leaves
    note = ((8, 2 * rank), f32)
    dma = pltpu.SemaphoreType.DMA


    uppers = (GROUP // 2 * 3 * (rank // 2), 2 * rank)

    def factored(grams, after, has_factor, has_low):
        return call(
            functools.partial(factor_kernel, len(grams), has_factor, has_low),
            [(packed, f32)] * (1 + has_factor) + [((1, *uppers), bf16)] * has_low,
            2.6,
            arrays=[*grams, after],
            scratch=work,
        )

    (gram,) = call(gram_kernel, [(packed, f32)], 1.0, arrays=[bases])
    message, token = call(
        child_kernel,
        [((GROUP + GROUP // 2, *packed[1:]), f32), note],
        0.8,
        arrays=[gram, leaf_transfer, top_transfer],
    )
    message_other = swapped(message, "leaf", 1)
    leaf_inverse, leaf_factor, low = factored([gram], token, True, True)
    halves, half_token = call(
        half_kernel,
        [((blocks, *square), bf16), note],
        2.7,
        scalars=[coupling_target],
        arrays=[jnp.transpose(couplings, (1, 2, 0)), leaf_factor],
        scratch=[turned, pltpu.VMEM((leaves, *square), bf16)],
    )
    middle_gram, top_gram, top_message, token = call(
        middle_kernel,
        [(packed, f32), (packed, f32), (uppers, f32), note],
        1.4,
        scalars=[spot],
        arrays=[message, message_other, half_token],
    )
    top_gram_other = swapped(top_message, "leaf", 2)
    middle_inverse, middle_factor = factored([middle_gram], token, True, False)
    table = joined_by_xor(held(low, half_token), "leaf", leaf_bits[:-2], middle_inverse)
    tables = [table, swapped(table, "leaf", 1 << leaf_bits[-2])]
    top_inverse, top_low = factored([top_gram, top_gram_other], table, False, True)
    tables += [swapped(one, "leaf", 1 << leaf_bits[-1]) for one in (held(table, top_inverse), tables[1])]
    top_table = joined_by_xor(top_low, "leaf", [bit + 2 for bit in quad_bits[:-1]], top_inverse)
    top_tables = [top_table, swapped(top_table, "leaf", 4 << quad_bits[-1])]
    leaf_bases, leaf_transfers, top_transfers, top_halves = call(
        output_kernel,
        [((share, *square), f32), ((leaves, *square), f32), ((GROUP, *square), f32), ((top_blocks, *square), bf16)],
        2.5,
        scalars=[spot, top_target],
        arrays=[
            bases,
            tables[1],
            top_couplings,
            top_low,
            leaf_factor,
            leaf_inverse,
            leaf_transfer,
            middle_factor,
            middle_inverse,
            top_transfer,
            top_inverse,
        ],
        scratch=[pltpu.VMEM((leaves, *square), bf16)],
    )
    (new_top_couplings,) = call(
        top_project_kernel,
        [((top_blocks, *square), bf16)],
        1.3,
        scalars=[top_right],
        arrays=[top_halves, *top_tables],
        scratch=[pltpu.VMEM((leaves * sum(one.shape[0] for one in top_tables), *square), bf16)],
    )
    ready = [leaf_bases, leaf_transfers, top_transfers, new_top_couplings]
    leaf_bases, leaf_transfers, top_transfers, new_top_couplings, new_couplings = call(
        functools.partial(full_kernel, len(ready)),
        [(one.shape, one.dtype) for one in ready] + [((rank, rank, blocks), bf16)],
        3.5,
        scalars=[source],
        arrays=[halves, *ready, *tables],
        scratch=[
            pltpu.VMEM((rank, rank, blocks), bf16),
            turned,
            pltpu.VMEM((leaves * sum(one.shape[0] for one in tables), *square), bf16),
            dma((len(ready) + CHUNKS,)),
        ],
        far_outs=len(ready) + 1,
    )
    new_couplings = jnp.transpose(new_couplings, (2, 0, 1))
    return (leaf_bases, leaf_transfers, top_transfers, new_couplings, new_top_couplings)


def solution(mesh):
    in_specs = (
        P("leaf", None, None),
        P("leaf", None, None),
        P("leaf", None, None),
        P(("leaf", "near"), None, None),
        P(("leaf", "near")),
        P(("leaf", "near"), None),
        P(("leaf", "near")),
        P(("leaf", "near"), None, None),
        P(("leaf", "near")),
        P(("leaf", "near")),
    )
    out_specs = (
        P(("leaf", "near"), None, None),
        P("leaf", None, None),
        P("leaf", None, None),
        P(("leaf", "near"), None, None),
        P(("leaf", "near"), None, None),
    )
    return jax.shard_map(
        on_device, mesh=mesh, in_specs=in_specs, out_specs=out_specs, check_vma=False
    )
```

```python
import functools

import jax
import jax.numpy as jnp
from jax import lax
from jax.experimental import pallas as pl
from jax.experimental.pallas import tpu as pltpu
from jax.sharding import PartitionSpec as P

exact = lax.Precision.HIGHEST
f32 = jnp.float32
bf16 = jnp.bfloat16
BLOCK = 8
GROUP = 4
PITCH_EXTRA = 8
CHUNKS = 4
VMEM_LIMIT = 48 * 2**20
FLOPS = 1e9


def swapped(value, axis, mask):
    pairs = [(source, source ^ mask) for source in range(lax.axis_size(axis))]
    return lax.ppermute(value, axis, pairs)


def join_kernel(first, second, after, out):
    out[: first.shape[0]] = first[...]
    out[first.shape[0] :] = second[...]


def hold_kernel(value, after, out):
    out[...] = value[...]


def held(value, after):
    return call(hold_kernel, [(value.shape, value.dtype)], 0.1, arrays=[value, after])[0]


def joined_by_xor(value, axis, bits, after):
    for bit in bits:
        other = swapped(value, axis, 1 << bit)
        shape = (2 * value.shape[0], *value.shape[1:])
        (value,) = call(join_kernel, [(shape, value.dtype)], 0.2, arrays=[value, other, after])
    return value


def place_of(difference, bits):
    place = jnp.zeros_like(difference)
    for order, bit in enumerate(bits):
        place = place | (((difference >> bit) & 1) << order)
    return place


def dot_nn(a, b):
    return jnp.dot(a, b, precision=exact, preferred_element_type=f32)


def dot_tn(a, b):
    return lax.dot_general(a, b, (((0,), (0,)), ((), ())), precision=exact, preferred_element_type=f32)


def near_nn(a, b):
    return jnp.dot(a, b, precision=lax.Precision.HIGH, preferred_element_type=f32)


def near_nt(a, b):
    return lax.dot_general(
        a, b, (((1,), (1,)), ((), ())), precision=lax.Precision.HIGH, preferred_element_type=f32
    )


def low_nn(a, b):
    return jnp.dot(a, b, preferred_element_type=f32)


def low_nt(a, b):
    return lax.dot_general(a, b, (((1,), (1,)), ((), ())), preferred_element_type=f32)


def eliminate(work, factor, inverse):
    rank = work.shape[1] // 2
    middle = rank // 2
    shape = (2 * GROUP, 2 * rank)
    lanes = lax.broadcasted_iota(jnp.int32, shape, 1)
    odd = lax.broadcasted_iota(jnp.int32, shape, 0) // GROUP
    upper = odd == 0
    column = lanes % rank
    side = lanes - column

    def pick(rows, index):
        return jnp.take_along_axis(rows, index, axis=1)

    def span(pair):
        return pl.ds(2 * GROUP * pair, 2 * GROUP)

    for start in range(0, rank, BLOCK):
        inside = (column >= start) & (column < start + BLOCK)
        rows = []
        for pair in range(start // 2, (start + BLOCK) // 2):
            both = work[span(pair), :]
            turned = pltpu.roll(both, GROUP, axis=0)
            rows += [jnp.where(upper, both, turned), jnp.where(upper, turned, both)]
        done = [(column == start + a).astype(f32) for a in range(BLOCK)]
        entry = [[pick(rows[a], side + (start + b)) if b >= a else None for b in range(BLOCK)] for a in range(BLOCK)]
        scaled = []
        for a in range(BLOCK):
            pivot = pltpu.reciprocal(entry[a][a], approx=True)
            scaled.append(rows[a] * pivot)
            for b in range(a + 1, BLOCK):
                share = entry[a][b] * pivot
                for c in range(b, BLOCK):
                    entry[b][c] = entry[b][c] - share * entry[a][c]
                rows[b] = rows[b] - share * rows[a]
                done[b] = done[b] - share * done[a]
        mixed = [jnp.where(inside, done[a], rows[a]) for a in range(BLOCK)]
        for pair in range((start + BLOCK) // 2, (middle if start < middle else rank) // 2):
            total = jnp.where(inside, 0.0, work[span(pair), :])
            index = side + odd + 2 * pair
            for a in range(BLOCK):
                total = total - pick(scaled[a], index) * mixed[a]
            work[span(pair), :] = total
        for a in range(0, BLOCK, 2):
            pair = (start + a) // 2
            row = odd + 2 * pair
            scale = lax.rsqrt(jnp.where(upper, entry[a][a], entry[a + 1][a + 1]))
            factor[span(pair), :] = jnp.where(
                column >= row, jnp.where(upper, rows[a], rows[a + 1]) * scale, 0.0
            )
            inverse[span(pair), :] = jnp.where(
                column <= row, jnp.where(upper, mixed[a], mixed[a + 1]) * scale, 0.0
            )
        if start + BLOCK == middle:
            update_second_half(work, factor, inverse)


def update_second_half(work, factor, inverse):
    rank = work.shape[1] // 2
    middle = rank // 2
    shape = (middle, 2 * rank)
    lanes = lax.broadcasted_iota(jnp.int32, shape, 1)
    early = lanes % rank < middle
    for g in range(GROUP):
        above = pl.ds(g, middle, stride=GROUP)
        below = pl.ds(GROUP * middle + g, middle, stride=GROUP)
        rows = jnp.where(early, inverse[above, :], factor[above, :])
        product = dot_tn(rows, rows)
        taken = jnp.where(lanes < rank, product[middle:rank, :], product[rank + middle :, :])
        work[below, :] = jnp.where(early, 0.0, work[below, :]) - taken


def matrix_pair(work, group):
    return pl.ds(group, work.shape[1] // 2, stride=GROUP)


def side_by_side(left, right):
    return jnp.concatenate([left, right], axis=1)


def pack_upper(pairs, out):
    rank = pairs[0].shape[0]
    half = rank // 2
    right = lax.broadcasted_iota(jnp.int32, (half, 2 * rank), 1) % rank >= half
    for n in range(GROUP // 2):
        first, second = pairs[2 * n], pairs[2 * n + 1]
        start = 3 * half * n
        out[start : start + half, :] = first[:half].astype(out.dtype)
        out[start + half : start + 2 * half, :] = second[:half].astype(out.dtype)
        turned = pltpu.roll(second[half:], 2 * rank - half, axis=1)
        out[start + 2 * half : start + 3 * half, :] = jnp.where(right, first[half:], turned).astype(out.dtype)


def unpack_upper(message):
    rank = message.shape[-1] // 2
    half = rank // 2
    right = lax.broadcasted_iota(jnp.int32, (half, 2 * rank), 1) % rank >= half
    pairs = []
    for n in range(GROUP // 2):
        start = 3 * half * n
        shared = message[start + 2 * half : start + 3 * half, :].astype(f32)
        for k, lower in enumerate((shared, pltpu.roll(shared, half, axis=1))):
            upper = message[start + k * half : start + (k + 1) * half, :]
            lower = jnp.where(right, lower, 0.0).astype(upper.dtype)
            pairs.append(jnp.concatenate([upper, lower], axis=0))
    return pairs


def gram_kernel(bases, gram):
    for g in range(GROUP):
        left, right = bases[g], bases[g + GROUP]
        gram[g] = side_by_side(dot_tn(left, left), dot_tn(right, right))


def congruent(gram, left, right):
    rank = gram.shape[0]
    first = dot_tn(left, dot_nn(gram[:, :rank], left))
    second = dot_tn(right, dot_nn(gram[:, rank:], right))
    return side_by_side(first, second)


def child_kernel(gram, transfer, top, message, token):
    token[...] = jnp.zeros_like(token)
    for g in range(GROUP):
        message[g] = congruent(gram[g], transfer[g], transfer[g + GROUP])
    for n in range(GROUP // 2):
        message[GROUP + n] = side_by_side(top[2 * n], top[2 * n + 1])


def middle_kernel(spot, mine, other, after, middle_gram, top_gram, message, token):
    rank = middle_gram.shape[1]
    token[...] = jnp.zeros_like(token)
    first = spot[1] == 0
    grams = []
    for g in range(GROUP):
        lanes = slice(g % 2 * rank, (g % 2 + 1) * rank)
        own, sibling = mine[GROUP + g // 2][:, lanes], other[GROUP + g // 2][:, lanes]
        both = mine[g] + other[g]
        middle_gram[g] = both
        grams.append(congruent(both, jnp.where(first, own, sibling), jnp.where(first, sibling, own)))
        top_gram[g] = grams[g]
    pack_upper(grams, message)


def factor_kernel(terms, has_factor, has_low, *refs):
    grams, refs = refs[:terms], refs[terms + 1 :]
    outs, (work, factor, inverse) = refs[:-3], refs[-3:]
    more = unpack_upper(grams[1]) if terms == 2 else None
    for g in range(GROUP):
        work[matrix_pair(work, g), :] = grams[0][g] if more is None else grams[0][g] + more[g]
    eliminate(work, factor, inverse)
    pairs = [factor[matrix_pair(work, g), :] for g in range(GROUP)]
    if has_low:
        pack_upper(pairs, outs[-1].at[0])
    for g in range(GROUP):
        outs[0][g] = inverse[matrix_pair(work, g), :]
        if has_factor:
            outs[1][g] = pairs[g]


def half_kernel(target, couplings, low, halves, token, turned, table):
    rank, _, count = couplings.shape
    pitch = turned.shape[0] // rank
    token[...] = jnp.zeros_like(token)
    for g in range(GROUP):
        both = low[g].astype(bf16)
        table[g] = both[:, :rank]
        table[g + GROUP] = both[:, rank:]
    for m in range(rank):
        turned[m * pitch : m * pitch + count, :] = couplings[m].astype(f32).T
    for r in range(count):
        block = turned[pl.ds(r, rank, stride=pitch), :].astype(bf16)
        halves[r] = low_nn(table[target[r]], block).astype(bf16)


def output_kernel(
    spot,
    target,
    bases,
    after,
    top_couplings,
    top_low,
    leaf_factor,
    leaf_inverse,
    leaf_transfer,
    middle_factor,
    middle_inverse,
    top_transfer,
    top_inverse,
    leaf_bases,
    leaf_transfers,
    top_transfers,
    top_halves,
    table,
):
    rank = bases.shape[2]
    share = leaf_bases.shape[0]
    unpack(top_low, table, 0, False)
    for r in range(top_couplings.shape[0]):
        top_halves[r] = low_nn(table[target[r]], top_couplings[r]).astype(bf16)
    for n, lanes in enumerate((slice(0, rank), slice(rank, 2 * rank))):
        for g in range(GROUP):
            place = n * GROUP + g
            piece = near_nn(leaf_factor[g][:, lanes], leaf_transfer[place])
            leaf_transfers[place] = near_nt(piece, middle_inverse[g][:, lanes])
    for g in range(GROUP):
        left, right = (jnp.where(spot[1] == 0, both[:, :rank], both[:, rank:]) for both in (middle_factor[g], top_inverse[g]))
        top_transfers[g] = near_nt(near_nn(left, top_transfer[g]), right)
    for k in range(share):
        place = spot[0] * share + k
        both = leaf_inverse[place % GROUP]
        both = jnp.where(place < GROUP, both[:, :rank], both[:, rank:])
        leaf_bases[k] = near_nt(bases[place], both)


def shares(count, steps):
    edges = [count * k // steps for k in range(steps + 1)]
    return [range(low, high) for low, high in zip(edges[:-1], edges[1:])]


def unpack(packed, table, base, turn):
    count, rank = packed.shape[0], table.shape[2]

    def step(n, carry):
        for g, both in enumerate(unpack_upper(packed.at[n])):
            place = base + 2 * GROUP * n + g
            if turn:
                both = both.T
                table[place] = both[:rank]
                table[place + GROUP] = both[rank:]
            else:
                table[place] = both[:, :rank]
                table[place + GROUP] = both[:, rank:]
        return carry

    lax.fori_loop(0, count, step, 0, unroll=min(count, 4))


def unpack_all(packed, table, turn):
    base = 0
    for one in packed:
        unpack(one, table, base, turn)
        base += 2 * GROUP * one.shape[0]


def full_kernel(ready, source, halves, *rest):
    near, rest = rest[:ready], rest[ready:]
    far, rest = rest[-5 - ready : -5], rest[: -5 - ready] + rest[-5:]
    packed, (out_far, out, turned, table, left) = rest[:-5], rest[-5:]
    count, rank, _ = halves.shape
    pitch = turned.shape[0] // rank
    copies = [pltpu.make_async_copy(near[n], far[n], left.at[n]) for n in range(ready)]
    for copy in copies:
        copy.start()
    unpack_all(packed, table, True)
    for r in range(count):
        turned[pl.ds(r, rank, stride=pitch), :] = low_nn(halves[r], table[source[r]])
    for k, part in enumerate(shares(rank, CHUNKS)):
        for m in part:
            out[m] = turned[m * pitch : m * pitch + count, :].T.astype(bf16)
        place = pl.ds(part.start, len(part))
        copies.append(pltpu.make_async_copy(out.at[place], out_far.at[place], left.at[ready + k]))
        copies[-1].start()
    for copy in copies:
        copy.wait()


def top_project_kernel(source, halves, *rest):
    packed, (out, table) = rest[:-2], rest[-2:]
    unpack_all(packed, table, False)
    for r in range(halves.shape[0]):
        out[r] = low_nt(halves[r], table[source[r]]).astype(bf16)


vmem = pl.BlockSpec(memory_space=pltpu.VMEM)
smem = pl.BlockSpec(memory_space=pltpu.SMEM)
hbm = pl.BlockSpec(memory_space=pltpu.HBM)


def call(kernel, outs, microseconds, scalars=(), far=(), arrays=(), scratch=(), far_outs=0):
    return pl.pallas_call(
        kernel,
        out_shape=[jax.ShapeDtypeStruct(shape, dtype) for shape, dtype in outs],
        in_specs=[smem] * len(scalars) + [hbm] * len(far) + [vmem] * len(arrays),
        out_specs=[hbm] * far_outs + [vmem] * (len(outs) - far_outs),
        scratch_shapes=list(scratch),
        compiler_params=pltpu.CompilerParams(vmem_limit_bytes=VMEM_LIMIT),
        cost_estimate=pl.CostEstimate(flops=int(microseconds * FLOPS), bytes_accessed=0, transcendentals=0),
    )(*scalars, *far, *arrays)


def on_device(
    bases,
    leaf_transfer,
    top_transfer,
    couplings,
    coupling_target,
    coupling_dest,
    coupling_local,
    top_couplings,
    top_target,
    top_source,
):
    leaves, _, rank = bases.shape
    share = leaves // lax.axis_size("near")
    blocks, top_blocks = couplings.shape[0], top_couplings.shape[0]
    leaf_bits = list(range(lax.axis_size("leaf").bit_length() - 1))[::-1]
    quad_bits = [bit - 2 for bit in leaf_bits if bit >= 2]
    near_place, leaf_place = lax.axis_index("near"), lax.axis_index("leaf")
    parity = leaf_place % 2
    spot = jnp.stack([near_place, parity]).astype(jnp.int32)
    square = (rank, rank)
    packed = (GROUP, rank, 2 * rank)
    work = [pltpu.VMEM((rank * GROUP, 2 * rank), f32)] * 3
    turned = pltpu.VMEM((rank * (blocks + PITCH_EXTRA), rank), f32)

    source = place_of(coupling_dest[:, 0] ^ leaf_place, leaf_bits) * leaves + coupling_local
    top_right = place_of((top_source // leaves) ^ (leaf_place // 4), quad_bits) * leaves + top_source % leaves
    note = ((8, 2 * rank), f32)
    dma = pltpu.SemaphoreType.DMA


    uppers = (GROUP // 2 * 3 * (rank // 2), 2 * rank)

    def factored(grams, after, has_factor, has_low):
        return call(
            functools.partial(factor_kernel, len(grams), has_factor, has_low),
            [(packed, f32)] * (1 + has_factor) + [((1, *uppers), bf16)] * has_low,
            2.6,
            arrays=[*grams, after],
            scratch=work,
        )

    (gram,) = call(gram_kernel, [(packed, f32)], 1.0, arrays=[bases])
    message, token = call(
        child_kernel,
        [((GROUP + GROUP // 2, *packed[1:]), f32), note],
        0.8,
        arrays=[gram, leaf_transfer, top_transfer],
    )
    message_other = swapped(message, "leaf", 1)
    leaf_inverse, leaf_factor, low = factored([gram], token, True, True)
    halves, half_token = call(
        half_kernel,
        [((blocks, *square), bf16), note],
        2.7,
        scalars=[coupling_target],
        arrays=[jnp.transpose(couplings, (1, 2, 0)), leaf_factor],
        scratch=[turned, pltpu.VMEM((leaves, *square), bf16)],
    )
    middle_gram, top_gram, top_message, token = call(
        middle_kernel,
        [(packed, f32), (packed, f32), (uppers, f32), note],
        1.4,
        scalars=[spot],
        arrays=[message, message_other, half_token],
    )
    top_gram_other = swapped(top_message, "leaf", 2)
    middle_inverse, middle_factor = factored([middle_gram], token, True, False)
    table = joined_by_xor(held(low, half_token), "leaf", leaf_bits[:-2], middle_inverse)
    tables = [table, swapped(table, "leaf", 1 << leaf_bits[-2])]
    late = held(table, top_gram_other)
    top_inverse, top_low = factored([top_gram, top_gram_other], late, False, True)
    tables += [swapped(one, "leaf", 1 << leaf_bits[-1]) for one in (late, tables[1])]
    top_table = joined_by_xor(top_low, "leaf", [bit + 2 for bit in quad_bits[:-1]], top_inverse)
    top_tables = [top_table, swapped(top_table, "leaf", 4 << quad_bits[-1])]
    leaf_bases, leaf_transfers, top_transfers, top_halves = call(
        output_kernel,
        [((share, *square), f32), ((leaves, *square), f32), ((GROUP, *square), f32), ((top_blocks, *square), bf16)],
        2.5,
        scalars=[spot, top_target],
        arrays=[
            bases,
            tables[1],
            top_couplings,
            top_low,
            leaf_factor,
            leaf_inverse,
            leaf_transfer,
            middle_factor,
            middle_inverse,
            top_transfer,
            top_inverse,
        ],
        scratch=[pltpu.VMEM((leaves, *square), bf16)],
    )
    (new_top_couplings,) = call(
        top_project_kernel,
        [((top_blocks, *square), bf16)],
        1.3,
        scalars=[top_right],
        arrays=[top_halves, *top_tables],
        scratch=[pltpu.VMEM((leaves * sum(one.shape[0] for one in top_tables), *square), bf16)],
    )
    ready = [leaf_bases, leaf_transfers, top_transfers, new_top_couplings]
    leaf_bases, leaf_transfers, top_transfers, new_top_couplings, new_couplings = call(
        functools.partial(full_kernel, len(ready)),
        [(one.shape, one.dtype) for one in ready] + [((rank, rank, blocks), bf16)],
        3.5,
        scalars=[source],
        arrays=[halves, *ready, *tables],
        scratch=[
            pltpu.VMEM((rank, rank, blocks), bf16),
            turned,
            pltpu.VMEM((leaves * sum(one.shape[0] for one in tables), *square), bf16),
            dma((len(ready) + CHUNKS,)),
        ],
        far_outs=len(ready) + 1,
    )
    new_couplings = jnp.transpose(new_couplings, (2, 0, 1))
    return (leaf_bases, leaf_transfers, top_transfers, new_couplings, new_top_couplings)


def solution(mesh):
    in_specs = (
        P("leaf", None, None),
        P("leaf", None, None),
        P("leaf", None, None),
        P(("leaf", "near"), None, None),
        P(("leaf", "near")),
        P(("leaf", "near"), None),
        P(("leaf", "near")),
        P(("leaf", "near"), None, None),
        P(("leaf", "near")),
        P(("leaf", "near")),
    )
    out_specs = (
        P(("leaf", "near"), None, None),
        P("leaf", None, None),
        P("leaf", None, None),
        P(("leaf", "near"), None, None),
        P(("leaf", "near"), None, None),
    )
    return jax.shard_map(
        on_device, mesh=mesh, in_specs=in_specs, out_specs=out_specs, check_vma=False
    )
```

```python
import functools

import jax
import jax.numpy as jnp
from jax import lax
from jax.experimental import pallas as pl
from jax.experimental.pallas import tpu as pltpu
from jax.sharding import PartitionSpec as P

exact = lax.Precision.HIGHEST
f32 = jnp.float32
bf16 = jnp.bfloat16
BLOCK = 8
GROUP = 4
PITCH_EXTRA = 8
CHUNKS = 4
VMEM_LIMIT = 48 * 2**20
FLOPS = 1e9


def swapped(value, axis, mask):
    pairs = [(source, source ^ mask) for source in range(lax.axis_size(axis))]
    return lax.ppermute(value, axis, pairs)


def join_kernel(first, second, after, out):
    out[: first.shape[0]] = first[...]
    out[first.shape[0] :] = second[...]


def hold_kernel(value, after, out):
    out[...] = value[...]


def held(value, after):
    return call(hold_kernel, [(value.shape, value.dtype)], 0.1, arrays=[value, after])[0]


def joined_by_xor(value, axis, bits, after):
    for bit in bits:
        other = swapped(value, axis, 1 << bit)
        shape = (2 * value.shape[0], *value.shape[1:])
        (value,) = call(join_kernel, [(shape, value.dtype)], 0.2, arrays=[value, other, after])
    return value


def place_of(difference, bits):
    place = jnp.zeros_like(difference)
    for order, bit in enumerate(bits):
        place = place | (((difference >> bit) & 1) << order)
    return place


def dot_nn(a, b):
    return jnp.dot(a, b, precision=exact, preferred_element_type=f32)


def dot_tn(a, b):
    return lax.dot_general(a, b, (((0,), (0,)), ((), ())), precision=exact, preferred_element_type=f32)


def near_nn(a, b):
    return jnp.dot(a, b, precision=lax.Precision.HIGH, preferred_element_type=f32)


def near_nt(a, b):
    return lax.dot_general(
        a, b, (((1,), (1,)), ((), ())), precision=lax.Precision.HIGH, preferred_element_type=f32
    )


def low_nn(a, b):
    return jnp.dot(a, b, preferred_element_type=f32)


def low_nt(a, b):
    return lax.dot_general(a, b, (((1,), (1,)), ((), ())), preferred_element_type=f32)


def eliminate(work, factor, inverse):
    rank = work.shape[1] // 2
    middle = rank // 2
    shape = (2 * GROUP, 2 * rank)
    lanes = lax.broadcasted_iota(jnp.int32, shape, 1)
    odd = lax.broadcasted_iota(jnp.int32, shape, 0) // GROUP
    upper = odd == 0
    column = lanes % rank
    side = lanes - column

    def pick(rows, index):
        return jnp.take_along_axis(rows, index, axis=1)

    def span(pair):
        return pl.ds(2 * GROUP * pair, 2 * GROUP)

    for start in range(0, rank, BLOCK):
        inside = (column >= start) & (column < start + BLOCK)
        rows = []
        for pair in range(start // 2, (start + BLOCK) // 2):
            both = work[span(pair), :]
            turned = pltpu.roll(both, GROUP, axis=0)
            rows += [jnp.where(upper, both, turned), jnp.where(upper, turned, both)]
        done = [(column == start + a).astype(f32) for a in range(BLOCK)]
        entry = [[pick(rows[a], side + (start + b)) if b >= a else None for b in range(BLOCK)] for a in range(BLOCK)]
        scaled = []
        for a in range(BLOCK):
            pivot = pltpu.reciprocal(entry[a][a], approx=True)
            scaled.append(rows[a] * pivot)
            for b in range(a + 1, BLOCK):
                share = entry[a][b] * pivot
                for c in range(b, BLOCK):
                    entry[b][c] = entry[b][c] - share * entry[a][c]
                rows[b] = rows[b] - share * rows[a]
                done[b] = done[b] - share * done[a]
        mixed = [jnp.where(inside, done[a], rows[a]) for a in range(BLOCK)]
        for pair in range((start + BLOCK) // 2, (middle if start < middle else rank) // 2):
            total = jnp.where(inside, 0.0, work[span(pair), :])
            index = side + odd + 2 * pair
            for a in range(BLOCK):
                total = total - pick(scaled[a], index) * mixed[a]
            work[span(pair), :] = total
        for a in range(0, BLOCK, 2):
            pair = (start + a) // 2
            row = odd + 2 * pair
            scale = lax.rsqrt(jnp.where(upper, entry[a][a], entry[a + 1][a + 1]))
            factor[span(pair), :] = jnp.where(
                column >= row, jnp.where(upper, rows[a], rows[a + 1]) * scale, 0.0
            )
            inverse[span(pair), :] = jnp.where(
                column <= row, jnp.where(upper, mixed[a], mixed[a + 1]) * scale, 0.0
            )
        if start + BLOCK == middle:
            update_second_half(work, factor, inverse)


def update_second_half(work, factor, inverse):
    rank = work.shape[1] // 2
    middle = rank // 2
    shape = (middle, 2 * rank)
    lanes = lax.broadcasted_iota(jnp.int32, shape, 1)
    early = lanes % rank < middle
    for g in range(GROUP):
        above = pl.ds(g, middle, stride=GROUP)
        below = pl.ds(GROUP * middle + g, middle, stride=GROUP)
        rows = jnp.where(early, inverse[above, :], factor[above, :])
        product = dot_tn(rows, rows)
        taken = jnp.where(lanes < rank, product[middle:rank, :], product[rank + middle :, :])
        work[below, :] = jnp.where(early, 0.0, work[below, :]) - taken


def matrix_pair(work, group):
    return pl.ds(group, work.shape[1] // 2, stride=GROUP)


def side_by_side(left, right):
    return jnp.concatenate([left, right], axis=1)


def pack_upper(pairs, out):
    rank = pairs[0].shape[0]
    half = rank // 2
    right = lax.broadcasted_iota(jnp.int32, (half, 2 * rank), 1) % rank >= half
    for n in range(GROUP // 2):
        first, second = pairs[2 * n], pairs[2 * n + 1]
        start = 3 * half * n
        out[start : start + half, :] = first[:half].astype(out.dtype)
        out[start + half : start + 2 * half, :] = second[:half].astype(out.dtype)
        turned = pltpu.roll(second[half:], 2 * rank - half, axis=1)
        out[start + 2 * half : start + 3 * half, :] = jnp.where(right, first[half:], turned).astype(out.dtype)


def unpack_upper(message):
    rank = message.shape[-1] // 2
    half = rank // 2
    right = lax.broadcasted_iota(jnp.int32, (half, 2 * rank), 1) % rank >= half
    pairs = []
    for n in range(GROUP // 2):
        start = 3 * half * n
        shared = message[start + 2 * half : start + 3 * half, :].astype(f32)
        for k, lower in enumerate((shared, pltpu.roll(shared, half, axis=1))):
            upper = message[start + k * half : start + (k + 1) * half, :]
            lower = jnp.where(right, lower, 0.0).astype(upper.dtype)
            pairs.append(jnp.concatenate([upper, lower], axis=0))
    return pairs


def gram_kernel(bases, gram):
    for g in range(GROUP):
        left, right = bases[g], bases[g + GROUP]
        gram[g] = side_by_side(dot_tn(left, left), dot_tn(right, right))


def congruent(gram, left, right):
    rank = gram.shape[0]
    first = dot_tn(left, dot_nn(gram[:, :rank], left))
    second = dot_tn(right, dot_nn(gram[:, rank:], right))
    return side_by_side(first, second)


def child_kernel(gram, transfer, top, message, token):
    token[...] = jnp.zeros_like(token)
    for g in range(GROUP):
        message[g] = congruent(gram[g], transfer[g], transfer[g + GROUP])
    for n in range(GROUP // 2):
        message[GROUP + n] = side_by_side(top[2 * n], top[2 * n + 1])


def middle_kernel(spot, mine, other, after, middle_gram, top_gram, message, token):
    rank = middle_gram.shape[1]
    token[...] = jnp.zeros_like(token)
    first = spot[1] == 0
    grams = []
    for g in range(GROUP):
        lanes = slice(g % 2 * rank, (g % 2 + 1) * rank)
        own, sibling = mine[GROUP + g // 2][:, lanes], other[GROUP + g // 2][:, lanes]
        both = mine[g] + other[g]
        middle_gram[g] = both
        grams.append(congruent(both, jnp.where(first, own, sibling), jnp.where(first, sibling, own)))
        top_gram[g] = grams[g]
    pack_upper(grams, message)


def factor_kernel(terms, has_factor, has_low, *refs):
    grams, refs = refs[:terms], refs[terms + 1 :]
    outs, (work, factor) = refs[:-2], refs[-2:]
    inverse = outs[0]
    more = unpack_upper(grams[1]) if terms == 2 else None
    for g in range(GROUP):
        work[matrix_pair(work, g), :] = grams[0][g] if more is None else grams[0][g] + more[g]
    eliminate(work, factor, inverse)
    pairs = [factor[matrix_pair(work, g), :] for g in range(GROUP)]
    if has_low:
        pack_upper(pairs, outs[-1].at[0])
    for g in range(GROUP):
        if has_factor:
            outs[1][g] = pairs[g]


def half_kernel(target, couplings, low, halves, token, turned, table):
    rank, _, count = couplings.shape
    pitch = turned.shape[0] // rank
    token[...] = jnp.zeros_like(token)
    for g in range(GROUP):
        both = low[g].astype(bf16)
        table[g] = both[:, :rank]
        table[g + GROUP] = both[:, rank:]
    for m in range(rank):
        turned[m * pitch : m * pitch + count, :] = couplings[m].astype(f32).T
    for r in range(count):
        block = turned[pl.ds(r, rank, stride=pitch), :].astype(bf16)
        halves[r] = low_nn(table[target[r]], block).astype(bf16)


def output_kernel(
    spot,
    target,
    bases,
    after,
    top_couplings,
    top_low,
    leaf_factor,
    leaf_inverse,
    leaf_transfer,
    middle_factor,
    middle_inverse,
    top_transfer,
    top_inverse,
    leaf_bases,
    leaf_transfers,
    top_transfers,
    top_halves,
    table,
):
    rank = bases.shape[2]
    share = leaf_bases.shape[0]
    unpack(top_low, table, 0, False)
    for r in range(top_couplings.shape[0]):
        top_halves[r] = low_nn(table[target[r]], top_couplings[r]).astype(bf16)
    for n, lanes in enumerate((slice(0, rank), slice(rank, 2 * rank))):
        for g in range(GROUP):
            place = n * GROUP + g
            piece = near_nn(leaf_factor[g][:, lanes], leaf_transfer[place])
            leaf_transfers[place] = near_nt(piece, middle_inverse[matrix_pair(middle_inverse, g), :][:, lanes])
    for g in range(GROUP):
        left, right = (jnp.where(spot[1] == 0, both[:, :rank], both[:, rank:]) for both in (middle_factor[g], top_inverse[matrix_pair(top_inverse, g), :]))
        top_transfers[g] = near_nt(near_nn(left, top_transfer[g]), right)
    for k in range(share):
        place = spot[0] * share + k
        both = leaf_inverse[matrix_pair(leaf_inverse, place % GROUP), :]
        both = jnp.where(place < GROUP, both[:, :rank], both[:, rank:])
        leaf_bases[k] = near_nt(bases[place], both)


def shares(count, steps):
    edges = [count * k // steps for k in range(steps + 1)]
    return [range(low, high) for low, high in zip(edges[:-1], edges[1:])]


def unpack(packed, table, base, turn):
    count, rank = packed.shape[0], table.shape[2]

    def step(n, carry):
        for g, both in enumerate(unpack_upper(packed.at[n])):
            place = base + 2 * GROUP * n + g
            if turn:
                both = both.T
                table[place] = both[:rank]
                table[place + GROUP] = both[rank:]
            else:
                table[place] = both[:, :rank]
                table[place + GROUP] = both[:, rank:]
        return carry

    lax.fori_loop(0, count, step, 0, unroll=min(count, 4))


def unpack_all(packed, table, turn):
    base = 0
    for one in packed:
        unpack(one, table, base, turn)
        base += 2 * GROUP * one.shape[0]


def full_kernel(ready, source, halves, *rest):
    near, rest = rest[:ready], rest[ready:]
    far, rest = rest[-5 - ready : -5], rest[: -5 - ready] + rest[-5:]
    packed, (out_far, out, turned, table, left) = rest[:-5], rest[-5:]
    count, rank, _ = halves.shape
    pitch = turned.shape[0] // rank
    copies = [pltpu.make_async_copy(near[n], far[n], left.at[n]) for n in range(ready)]
    for copy in copies:
        copy.start()
    unpack_all(packed, table, True)
    for r in range(count):
        turned[pl.ds(r, rank, stride=pitch), :] = low_nn(halves[r], table[source[r]])
    for k, part in enumerate(shares(rank, CHUNKS)):
        for m in part:
            out[m] = turned[m * pitch : m * pitch + count, :].T.astype(bf16)
        place = pl.ds(part.start, len(part))
        copies.append(pltpu.make_async_copy(out.at[place], out_far.at[place], left.at[ready + k]))
        copies[-1].start()
    for copy in copies:
        copy.wait()


def top_project_kernel(source, halves, *rest):
    packed, (out, table) = rest[:-2], rest[-2:]
    unpack_all(packed, table, False)
    for r in range(halves.shape[0]):
        out[r] = low_nt(halves[r], table[source[r]]).astype(bf16)


vmem = pl.BlockSpec(memory_space=pltpu.VMEM)
smem = pl.BlockSpec(memory_space=pltpu.SMEM)
hbm = pl.BlockSpec(memory_space=pltpu.HBM)


def call(kernel, outs, microseconds, scalars=(), far=(), arrays=(), scratch=(), far_outs=0):
    return pl.pallas_call(
        kernel,
        out_shape=[jax.ShapeDtypeStruct(shape, dtype) for shape, dtype in outs],
        in_specs=[smem] * len(scalars) + [hbm] * len(far) + [vmem] * len(arrays),
        out_specs=[hbm] * far_outs + [vmem] * (len(outs) - far_outs),
        scratch_shapes=list(scratch),
        compiler_params=pltpu.CompilerParams(vmem_limit_bytes=VMEM_LIMIT),
        cost_estimate=pl.CostEstimate(flops=int(microseconds * FLOPS), bytes_accessed=0, transcendentals=0),
    )(*scalars, *far, *arrays)


def on_device(
    bases,
    leaf_transfer,
    top_transfer,
    couplings,
    coupling_target,
    coupling_dest,
    coupling_local,
    top_couplings,
    top_target,
    top_source,
):
    leaves, _, rank = bases.shape
    share = leaves // lax.axis_size("near")
    blocks, top_blocks = couplings.shape[0], top_couplings.shape[0]
    leaf_bits = list(range(lax.axis_size("leaf").bit_length() - 1))[::-1]
    quad_bits = [bit - 2 for bit in leaf_bits if bit >= 2]
    near_place, leaf_place = lax.axis_index("near"), lax.axis_index("leaf")
    parity = leaf_place % 2
    spot = jnp.stack([near_place, parity]).astype(jnp.int32)
    square = (rank, rank)
    packed = (GROUP, rank, 2 * rank)
    work = [pltpu.VMEM((rank * GROUP, 2 * rank), f32)] * 2
    turned = pltpu.VMEM((rank * (blocks + PITCH_EXTRA), rank), f32)

    source = place_of(coupling_dest[:, 0] ^ leaf_place, leaf_bits) * leaves + coupling_local
    top_right = place_of((top_source // leaves) ^ (leaf_place // 4), quad_bits) * leaves + top_source % leaves
    note = ((8, 2 * rank), f32)
    dma = pltpu.SemaphoreType.DMA


    uppers = (GROUP // 2 * 3 * (rank // 2), 2 * rank)

    def factored(grams, after, has_factor, has_low):
        return call(
            functools.partial(factor_kernel, len(grams), has_factor, has_low),
            [((rank * GROUP, 2 * rank), f32)] + [(packed, f32)] * has_factor + [((1, *uppers), bf16)] * has_low,
            2.6,
            arrays=[*grams, after],
            scratch=work,
        )

    (gram,) = call(gram_kernel, [(packed, f32)], 1.0, arrays=[bases])
    message, token = call(
        child_kernel,
        [((GROUP + GROUP // 2, *packed[1:]), f32), note],
        0.8,
        arrays=[gram, leaf_transfer, top_transfer],
    )
    message_other = swapped(message, "leaf", 1)
    leaf_inverse, leaf_factor, low = factored([gram], token, True, True)
    halves, half_token = call(
        half_kernel,
        [((blocks, *square), bf16), note],
        2.7,
        scalars=[coupling_target],
        arrays=[jnp.transpose(couplings, (1, 2, 0)), leaf_factor],
        scratch=[turned, pltpu.VMEM((leaves, *square), bf16)],
    )
    middle_gram, top_gram, top_message, token = call(
        middle_kernel,
        [(packed, f32), (packed, f32), (uppers, f32), note],
        1.4,
        scalars=[spot],
        arrays=[message, message_other, half_token],
    )
    top_gram_other = swapped(top_message, "leaf", 2)
    middle_inverse, middle_factor = factored([middle_gram], token, True, False)
    table = joined_by_xor(held(low, half_token), "leaf", leaf_bits[:-2], middle_inverse)
    tables = [table, swapped(table, "leaf", 1 << leaf_bits[-2])]
    late = held(table, top_gram_other)
    top_inverse, top_low = factored([top_gram, top_gram_other], late, False, True)
    tables += [swapped(one, "leaf", 1 << leaf_bits[-1]) for one in (late, tables[1])]
    top_table = joined_by_xor(top_low, "leaf", [bit + 2 for bit in quad_bits[:-1]], top_inverse)
    top_tables = [top_table, swapped(top_table, "leaf", 4 << quad_bits[-1])]
    leaf_bases, leaf_transfers, top_transfers, top_halves = call(
        output_kernel,
        [((share, *square), f32), ((leaves, *square), f32), ((GROUP, *square), f32), ((top_blocks, *square), bf16)],
        2.5,
        scalars=[spot, top_target],
        arrays=[
            bases,
            tables[1],
            top_couplings,
            top_low,
            leaf_factor,
            leaf_inverse,
            leaf_transfer,
            middle_factor,
            middle_inverse,
            top_transfer,
            top_inverse,
        ],
        scratch=[pltpu.VMEM((leaves, *square), bf16)],
    )
    (new_top_couplings,) = call(
        top_project_kernel,
        [((top_blocks, *square), bf16)],
        1.3,
        scalars=[top_right],
        arrays=[top_halves, *top_tables],
        scratch=[pltpu.VMEM((leaves * sum(one.shape[0] for one in top_tables), *square), bf16)],
    )
    ready = [leaf_bases, leaf_transfers, top_transfers, new_top_couplings]
    leaf_bases, leaf_transfers, top_transfers, new_top_couplings, new_couplings = call(
        functools.partial(full_kernel, len(ready)),
        [(one.shape, one.dtype) for one in ready] + [((rank, rank, blocks), bf16)],
        3.5,
        scalars=[source],
        arrays=[halves, *ready, *tables],
        scratch=[
            pltpu.VMEM((rank, rank, blocks), bf16),
            turned,
            pltpu.VMEM((leaves * sum(one.shape[0] for one in tables), *square), bf16),
            dma((len(ready) + CHUNKS,)),
        ],
        far_outs=len(ready) + 1,
    )
    new_couplings = jnp.transpose(new_couplings, (2, 0, 1))
    return (leaf_bases, leaf_transfers, top_transfers, new_couplings, new_top_couplings)


def solution(mesh):
    in_specs = (
        P("leaf", None, None),
        P("leaf", None, None),
        P("leaf", None, None),
        P(("leaf", "near"), None, None),
        P(("leaf", "near")),
        P(("leaf", "near"), None),
        P(("leaf", "near")),
        P(("leaf", "near"), None, None),
        P(("leaf", "near")),
        P(("leaf", "near")),
    )
    out_specs = (
        P(("leaf", "near"), None, None),
        P("leaf", None, None),
        P("leaf", None, None),
        P(("leaf", "near"), None, None),
        P(("leaf", "near"), None, None),
    )
    return jax.shard_map(
        on_device, mesh=mesh, in_specs=in_specs, out_specs=out_specs, check_vma=False
    )
```
